32 devices in a mesh: group: 4 (over y, x), fsdp: 8 (over z, core).
Axes of the slice: x: 2, y: 2, z: 4, core: 2. Of those that a mesh axis runs over, the one named last changes fastest.
Arguments:
- hidden_input_slots: bfloat16 [256, 8192], P('group'), may hold values from -6 to 6
- base_weight: bfloat16 [8192, 14784], P('group', 'fsdp'), may hold values from -0.0625 to 0.0625
- adapter_a: bfloat16 [8192, 64], P('group'), may hold values from -0.0625 to 0.0625
- adapter_up_matrix: bfloat16 [64, 14784], P(None, 'fsdp'), may hold values from -0.75 to 0.75
- upstream: bfloat16 [256, 14784], P('group', 'fsdp'), may hold values from -6 to 6
- logp_new: float32 [4, 4, 16], P('group'), may hold values from -2 to -0.5
- logp_old: float32 [4, 4, 16], P('group'), may hold values from -2 to -0.5
- rewards: float32 [4, 4], P('group'), may hold values from -1.35 to 2.35
- comp_lengths: int32 [4, 4], P('group'), may hold values from 1 to 16, 40 in all within a row
- assignment: int32 [4, 4], P('group'), may hold values from 0 to 3, each once within a row
Outputs:
- projection_output: bfloat16 [256, 14784], P('group', 'fsdp')
- gradient_down_adapter: float32 [8192, 64], P('group')
- gradient_up_adapter: float32 [64, 14784], P('group', 'fsdp')
- loss_parts: float32 [4], P('group')
The draws below stay inside these ranges and needn't reach their ends.
Inputs may be any that keep to these rules, and one draw needn't show every extreme that they name: `comp_lengths`: every generator group has a completion of exactly 16 tokens. `assignment`: each generator group assigns exactly one completion to each trainer group.
All inputs are finite; a program needn't handle non-finite values.
Results may differ from the reference program's by a relative error of at most 0.0049.
Values may be sent and summed in bfloat16 or wider, within the bound.
No kernel may reach another device: no remote copies, remote signals or barrier semaphores. Data moves between devices by JAX's collectives and lax.ppermute only.
A program may use at most 128 MiB of HBM per device.

```python
import math
import jax
import jax.numpy as jnp
import numpy as np
from jax import lax

D = 8192
FFW = 14784
R = 64
LEN = 16
COMP = 16
TOKENS = 256
PROMPTS = 1
N_GROUP = 4


def draw_rewards(key, part):
    prompts = (jnp.arange(N_GROUP * N_GROUP, dtype=jnp.int32) // COMP).reshape(N_GROUP, N_GROUP)
    levels = jax.random.randint(jax.random.fold_in(key, 12), (PROMPTS,), 0, 5).astype(jnp.float32) / 4.0
    success = levels[prompts]
    uniform_draw = jax.random.uniform(jax.random.fold_in(key, 13), (N_GROUP, N_GROUP), dtype=jnp.float32)
    correct = (uniform_draw < success).astype(jnp.float32)
    row_scale = 1.0 + 2.0 * jnp.arange(N_GROUP).astype(jnp.float32)[:, None] / max(N_GROUP - 1, 1)
    noise = jax.random.truncated_normal(jax.random.fold_in(key, 14), -3.0, 3.0, (N_GROUP, N_GROUP), dtype=jnp.float32)
    return correct + 0.15 * row_scale * noise


def block_levels(key, shape, cuts, low, largest):
    gain, own = 1.0, jax.random.fold_in(key, 6)
    for position, blocks in cuts:
        heights = jnp.exp(jax.random.uniform(jax.random.fold_in(own, position), (blocks,), jnp.float32, low / len(cuts), largest / len(cuts)))
        gain = gain * jnp.repeat(heights, shape[position] // blocks).reshape([-1 if axis == position else 1 for axis in range(len(shape))])
    return gain


def profile(amount, total, bound, lean):
    loads = [(1 << 20) // math.isqrt(rank ** lean) + 1 for rank in range(2, amount + 1)]
    surplus, holding = total - bound - (amount - 1), [1] * (amount - 1)
    while surplus > 0:
        candidates = [i for i in range(amount - 1) if holding[i] < bound]
        pool, left = sum([loads[i] for i in candidates]), surplus
        for i in candidates:
            more = min(bound - holding[i], max(1, left * loads[i] // pool), surplus)
            holding[i] = holding[i] + more
            surplus = surplus - more
    return np.array([bound] + holding)


def uneven(key, count, total, most, slope):
    if count == 2:
        one = jax.random.randint(key, (), max(1, total - most), min(most, total - 1) + 1)
        return jnp.stack([one, total - one])
    sizes = jnp.asarray(profile(count, total, most, slope), jnp.int32)
    pairs = (count - 1) // 2
    giver, receiver = sizes[1:1 + 2 * pairs:2], sizes[2:2 + 2 * pairs:2]
    room = jnp.minimum(giver - 1, most - receiver)
    moved = jax.random.randint(jax.random.fold_in(key, 1), (pairs,), 0, 1 << 20) % (room + 1)
    sizes = sizes.at[1:1 + 2 * pairs:2].set(giver - moved).at[2:2 + 2 * pairs:2].set(receiver + moved)
    return sizes[jax.random.permutation(jax.random.fold_in(key, 2), count)]


def centred(rng, extent, scale, most, cuts=(), kind=jnp.bfloat16):
    loudness = block_levels(rng, extent, cuts, -0.22, 0.18) if cuts else 1.0
    array = jax.random.normal(rng, extent, jnp.float32) * scale * loudness
    return jnp.minimum(jnp.maximum(array, -most), most).astype(kind)


def setup_inputs(seed: int = 0) -> dict:
    keys = jax.random.split(jax.random.key(seed), 11)
    return {
        "hidden_input_slots": centred(keys[0], (TOKENS, D), 1.0, 6.0, ((0, 4),)),
        "base_weight": centred(keys[1], (D, FFW), D ** -0.5, 0.0625, ((0, 4), (1, 8))),
        "adapter_a": centred(keys[2], (D, R), D ** -0.5, 0.0625, ((0, 4),)),
        "adapter_up_matrix": centred(keys[3], (R, FFW), R ** -0.5, 0.75, ((1, 8),)),
        "upstream": centred(keys[4], (TOKENS, FFW), 1.0, 6.0, ((0, 4), (1, 8))),
        "logp_new": jnp.clip(-2.0 + 1.5 * jax.random.uniform(keys[5], (N_GROUP, N_GROUP, LEN), jnp.float32) ** block_levels(keys[5], (N_GROUP, N_GROUP, LEN), ((0, 4),), -0.2, 0.2), -2.0, -0.5),
        "logp_old": jnp.clip(-2.0 + 1.5 * jax.random.uniform(keys[6], (N_GROUP, N_GROUP, LEN), jnp.float32) ** block_levels(keys[6], (N_GROUP, N_GROUP, LEN), ((0, 4),), -0.2, 0.2), -2.0, -0.5),
        "rewards": draw_rewards(jax.random.fold_in(keys[10], 71), 0),
        "comp_lengths": jax.vmap(lambda own: uneven(own, N_GROUP, N_GROUP * LEN * 5 // 8, LEN, 1))(jax.random.split(keys[8], N_GROUP)).reshape((N_GROUP, N_GROUP)).astype(jnp.int32),
        "assignment": jax.vmap(lambda own: jax.random.permutation(own, N_GROUP))(jax.random.split(keys[9], N_GROUP)).reshape((N_GROUP, N_GROUP)).astype(jnp.int32),
    }


ADAPTER_SCALING = 0.25
SPREAD_FLOOR = 0.16

def prompt_table(prompt_row, count):
    return (prompt_row[:, None] == jnp.arange(count, dtype=jnp.int32)[None, :]).astype(jnp.float32)

def advantages(reward_row, onehot, reward_sums, reward_squares):
    reward_mean = reward_sums / COMP
    reward_var = reward_squares / COMP - reward_mean * reward_mean
    spread = jnp.sqrt(jnp.maximum(reward_var, SPREAD_FLOOR))
    centre = jnp.dot(onehot, reward_mean, precision=lax.Precision.HIGHEST)
    scaled = jnp.dot(onehot, spread, precision=lax.Precision.HIGHEST)
    return (reward_row - centre) / scaled

def reference(hidden_input_slots, base_weight, adapter_a, adapter_up_matrix, upstream, logp_new, logp_old, rewards, comp_lengths, assignment):
    flat_rewards = rewards.reshape(-1)
    prompt_row = (jnp.arange(N_GROUP * N_GROUP, dtype=jnp.int32) // COMP).astype(jnp.int32)
    onehot = prompt_table(prompt_row, PROMPTS)
    reward_sums = jnp.dot(flat_rewards, onehot, precision=lax.Precision.HIGHEST)
    reward_squares = jnp.dot(flat_rewards * flat_rewards, onehot, precision=lax.Precision.HIGHEST)
    advantage = advantages(flat_rewards, onehot, reward_sums, reward_squares).reshape(N_GROUP, N_GROUP)
    handover = (assignment[:, None, :] == jnp.arange(N_GROUP, dtype=jnp.int32)[None, :, None]).astype(jnp.float32)
    recv_old = jnp.einsum('jtk,jki->tji', handover, logp_old, precision=lax.Precision.HIGHEST)
    recv_adv = jnp.einsum('jtk,jk->tj', handover, advantage, precision=lax.Precision.HIGHEST)
    recv_len = jnp.einsum('jtk,jk->tj', handover, comp_lengths.astype(jnp.float32), precision=lax.Precision.HIGHEST)
    positions = jnp.arange(LEN).astype(jnp.float32)
    live_mask = positions[None, None, :] < recv_len[:, :, None]
    prob_ratio = jnp.exp(logp_new - recv_old)
    token_coef = jnp.where(live_mask, -(recv_adv[:, :, None] * prob_ratio) / (recv_len[:, :, None] * COMP), 0.0)
    loss_parts = lax.optimization_barrier(jnp.sum(token_coef, axis=(1, 2)))
    output_gradient = (token_coef.reshape(TOKENS, 1) * upstream.astype(jnp.float32)).astype(jnp.bfloat16)
    reduced_rank_product = jnp.dot(hidden_input_slots, adapter_a, preferred_element_type=jnp.float32).astype(jnp.bfloat16)
    frozen_base_term = jnp.dot(hidden_input_slots, base_weight, preferred_element_type=jnp.float32)
    projection_output = (frozen_base_term + ADAPTER_SCALING * jnp.dot(reduced_rank_product, adapter_up_matrix, preferred_element_type=jnp.float32)).astype(jnp.bfloat16)
    gradient_up_adapter = ADAPTER_SCALING * jnp.dot(reduced_rank_product.T, output_gradient, preferred_element_type=jnp.float32)
    backward_lowrank = jnp.dot(output_gradient, adapter_up_matrix.T, preferred_element_type=jnp.float32).astype(jnp.bfloat16)
    gradient_down_adapter = ADAPTER_SCALING * jnp.dot(hidden_input_slots.T, backward_lowrank, preferred_element_type=jnp.float32)
    return (projection_output, gradient_down_adapter, gradient_up_adapter, loss_parts)
```

```python
import jax
import jax.numpy as jnp
from jax import lax
from jax.sharding import PartitionSpec as P

COMP = 16


ADAPTER_SCALING = 0.25
SPREAD_FLOOR = 0.16
F32 = jnp.float32
BF16 = jnp.bfloat16


def swap(array, axis, distance):
    size = lax.axis_size(axis)
    return lax.ppermute(array, axis, [(i, i ^ distance) for i in range(size)])


def is_power(number):
    return number & (number - 1) == 0


def sum_over_pairs(partial):
    size = lax.axis_size("fsdp")
    if not is_power(size):
        return lax.psum(partial, "fsdp", axis_index_groups=[[i for i in range(size) if i % 2 == r] for r in range(2)])
    parts = [partial] + [swap(partial, "fsdp", d) for d in range(2, size, 2)]
    while len(parts) > 1:
        parts = [parts[i] + parts[i + 1] for i in range(0, len(parts), 2)]
    return parts[0]


def coefficients(table, logp_new, own_group):
    groups = logp_new.shape[0]
    length = logp_new.shape[1]
    prompts = max(groups * groups // COMP, 1)
    order = own_group ^ jnp.arange(groups, dtype=jnp.int32)
    pick = (order[:, None] == jnp.arange(groups, dtype=jnp.int32)[None, :]).astype(F32)
    rows = jnp.sum(jnp.where(pick[:, :, None, None] > 0, table[None], 0.0), axis=1)
    rewards = rows[:, :, length]
    flat = (jnp.arange(groups * groups, dtype=jnp.int32) // COMP).reshape(groups, groups)
    onehot = flat[:, :, None] == jnp.arange(prompts, dtype=jnp.int32)
    sums = jnp.sum(jnp.where(onehot, rewards[:, :, None], 0.0), axis=(0, 1))
    squares = jnp.sum(jnp.where(onehot, (rewards * rewards)[:, :, None], 0.0), axis=(0, 1))
    mean = sums / COMP
    spread = jnp.sqrt(jnp.maximum(squares / COMP - mean * mean, SPREAD_FLOOR))
    centre = jnp.sum(jnp.where(onehot, mean, 0.0), axis=-1)
    scaled = jnp.sum(jnp.where(onehot, spread, 0.0), axis=-1)
    advantage = (rewards - centre) / scaled
    mine = rows[:, :, length + 2] == own_group.astype(F32)
    recv_old = jnp.sum(jnp.where(mine[:, :, None], rows[:, :, :length], 0.0), axis=1)
    recv_adv = jnp.sum(jnp.where(mine, advantage, 0.0), axis=1)
    recv_len = jnp.sum(jnp.where(mine, rows[:, :, length + 1], 0.0), axis=1)
    positions = jnp.arange(length).astype(F32)
    live_mask = positions[None, :] < recv_len[:, None]
    prob_ratio = jnp.exp(logp_new - recv_old)
    return jnp.where(live_mask, -(recv_adv[:, None] * prob_ratio) / (recv_len[:, None] * COMP), 0.0)


def dot(a, b, dims=((1,), (0,))):
    return lax.dot_general(a, b, (dims, ((), ())), preferred_element_type=F32)


def on_device(
    hidden_input_slots,
    base_weight,
    adapter_a,
    adapter_up_matrix,
    upstream,
    logp_new,
    logp_old,
    rewards,
    comp_lengths,
    assignment,
):
    groups = lax.axis_size("group")
    own_group = lax.axis_index("group")
    core = lax.axis_index("fsdp") % 2
    depth = base_weight.shape[0]
    half = depth // 2
    rank = adapter_a.shape[1]
    others = range(1, groups)

    pieces = {
        d: lax.dynamic_slice_in_dim(hidden_input_slots, (own_group ^ d) * depth + core * half, half, 1)
        for d in others
    }
    got = {d: swap(pieces[d], "group", d) for d in others}
    small = jnp.concatenate(
        [
            logp_old[0],
            rewards[0][:, None],
            comp_lengths[0].astype(F32)[:, None],
            assignment[0].astype(F32)[:, None],
        ],
        axis=1,
    )
    table = jnp.stack([small] + [swap(small, "group", d) for d in others])
    token_coef = coefficients(table, logp_new[0], own_group)
    loss_part = jnp.sum(token_coef)[None]
    coef = token_coef.reshape(-1, 1)

    back = dot(upstream, adapter_up_matrix, ((1,), (1,)))
    back = sum_over_pairs(back)
    back = back + swap(back, "fsdp", 1)

    own_hidden = lax.dynamic_slice_in_dim(hidden_input_slots, own_group * depth, depth, 1)
    full = {0: own_hidden}
    theirs = swap(jnp.concatenate([got[d] for d in others], axis=0), "fsdp", 1)
    rows = own_hidden.shape[0]
    for d in others:
        a, b = got[d], theirs[(d - 1) * rows : d * rows]
        first = core == 0
        full[d] = jnp.concatenate([jnp.where(first, a, b), jnp.where(first, b, a)], axis=1)

    scaled_back = coef * back
    low_terms = {d: dot(full[d], adapter_a) for d in range(groups)}
    low = low_terms[0]
    backs = {0: scaled_back}
    for d in others:
        came = swap(jnp.concatenate([low_terms[d], scaled_back], axis=1), "group", d)
        low = low + came[:, :rank]
        backs[d] = came[:, rank:]
    low = low.astype(BF16)

    output = dot(full[0], base_weight) + ADAPTER_SCALING * dot(low, adapter_up_matrix)
    for d in others:
        output = output + swap(dot(full[d], base_weight).astype(BF16), "group", d).astype(F32)
    projection_output = output.astype(BF16)

    hidden_all = jnp.concatenate([full[d] for d in range(groups)], axis=0)
    back_all = jnp.concatenate([backs[d] for d in range(groups)], axis=0).astype(BF16)
    gradient_down = ADAPTER_SCALING * dot(hidden_all, back_all, ((0,), (0,)))

    output_gradient = (coef * upstream.astype(F32)).astype(BF16)
    up_term = ADAPTER_SCALING * dot(low, output_gradient, ((0,), (0,)))
    share = rank // groups
    gradient_up = lax.dynamic_slice_in_dim(up_term, own_group * share, share, 0)
    for d in others:
        term = lax.dynamic_slice_in_dim(up_term, (own_group ^ d) * share, share, 0).astype(BF16)
        gradient_up = gradient_up + swap(term, "group", d).astype(F32)
    return (projection_output, gradient_down, gradient_up, loss_part)


def solution(mesh):
    return jax.shard_map(
        on_device,
        mesh=mesh,
        in_specs=(
            P("group", None),
            P("group", "fsdp"),
            P("group", None),
            P(None, "fsdp"),
            P("group", "fsdp"),
            P("group", None, None),
            P("group", None, None),
            P("group", None),
            P("group", None),
            P("group", None),
        ),
        out_specs=(P("group", "fsdp"), P("group", None), P("group", "fsdp"), P("group")),
        check_vma=False,
    )
```

```python
import functools

import jax
import jax.numpy as jnp
from jax import lax
from jax.experimental import pallas as pl
from jax.experimental.pallas import tpu as pltpu
from jax.sharding import PartitionSpec as P

COMP = 16


ADAPTER_SCALING = 0.25
SPREAD_FLOOR = 0.16
F32 = jnp.float32
BF16 = jnp.bfloat16
LANES = 128
BLOCK = 8
STEP = 512
NT = (((1,), (1,)), ((), ()))
TN = (((0,), (0,)), ((), ()))
VMEM = pl.BlockSpec(memory_space=pltpu.VMEM)
SMEM = pl.BlockSpec(memory_space=pltpu.SMEM)
HBM = pl.BlockSpec(memory_space=pltpu.HBM)
ANY = pl.BlockSpec(memory_space=pl.ANY)


def swap(array, axis, distance):
    size = lax.axis_size(axis)
    return lax.ppermute(array, axis, [(i, i ^ distance) for i in range(size)])


def sum_over_pairs(partial):
    size = lax.axis_size("fsdp")
    if size & (size - 1):
        same = [[i for i in range(size) if i % 2 == r] for r in range(2)]
        return lax.psum(partial, "fsdp", axis_index_groups=same)
    parts = [partial] + [swap(partial, "fsdp", d) for d in range(2, size, 2)]
    while len(parts) > 1:
        parts = [parts[i] + parts[i + 1] for i in range(0, len(parts), 2)]
    return parts[0]


def call(body, name, outs, ins, out_specs=None, scratch=(), limit=8, flops=0, moved=0):
    return pl.pallas_call(
        body,
        out_shape=outs,
        in_specs=ins,
        out_specs=[VMEM] * len(outs) if out_specs is None else out_specs,
        scratch_shapes=scratch,
        compiler_params=pltpu.CompilerParams(vmem_limit_bytes=limit << 20),
        cost_estimate=pl.CostEstimate(flops=flops, bytes_accessed=moved, transcendentals=0),
        name=name,
    )


def in_hbm(array):
    return pltpu.with_memory_space_constraint(array, pltpu.HBM)


def positions():
    own, member = lax.axis_index("group"), lax.axis_index("fsdp")
    return own, member, lax.rem(member, 2)


def pack_kernel(groups, depth, hidden_ref, old_hbm, reward_hbm, length_hbm, dest_hbm, *rest):
    messages, own_table, own_hidden = rest[: groups - 1], rest[groups - 1], rest[groups]
    old_ref, reward_ref, length_ref, dest_ref, sems, small_sems = rest[groups + 1 :]
    own, _, core = positions()
    half = depth // 2
    copies = []
    for d in reversed(range(1, groups)):
        start = pl.multiple_of((own ^ d) * depth + core * half, LANES)
        copies.append((hidden_ref.at[:, pl.ds(start, half)], messages[d - 1].at[:, :half]))
    copies.append((hidden_ref.at[:, pl.ds(pl.multiple_of(own * depth, LANES), depth)], own_hidden))
    copies = [pltpu.make_async_copy(a, b, sems.at[i]) for i, (a, b) in enumerate(copies)]
    small = ((old_hbm, old_ref), (reward_hbm, reward_ref), (length_hbm, length_ref), (dest_hbm, dest_ref))
    small = [pltpu.make_async_copy(a, b, small_sems.at[i]) for i, (a, b) in enumerate(small)]
    for copy in small + copies:
        copy.start()
    for copy in small:
        copy.wait()
    total, squares = jnp.float32(0), jnp.float32(0)
    for k in range(groups):
        total += reward_ref[0, k]
        squares += reward_ref[0, k] * reward_ref[0, k]
    old = old_ref[0]
    old = jnp.concatenate([old, jnp.zeros((groups, LANES - old.shape[1]), F32)], axis=1)
    for d in range(groups):
        line, reward, length = jnp.zeros((1, LANES), F32), jnp.float32(0), jnp.float32(0)
        for k in range(groups):
            chosen = dest_ref[0, k] == (own ^ d)
            line = jnp.where(chosen, old[k : k + 1], line)
            reward = jnp.where(chosen, reward_ref[0, k], reward)
            length = jnp.where(chosen, length_ref[0, k].astype(F32), length)
        lines = [line] + [jnp.full((1, LANES), x, F32) for x in (reward, length, total, squares)]
        value = jnp.concatenate(lines + [jnp.zeros((BLOCK - len(lines), LANES), F32)], axis=0)
        if d == 0:
            own_table[...] = value
            continue
        terms = []
        for _ in range(3):
            terms.append(value.astype(BF16).astype(F32))
            value = value - terms[-1]
        terms = jnp.concatenate(terms + [jnp.zeros((BLOCK, LANES), F32)], axis=0)
        messages[d - 1][: 4 * BLOCK, half:] = terms.astype(BF16)
    for copy in copies:
        copy.wait()


def back_kernel(upstream_hbm, up_hbm, upstream_ref, up_ref, back_ref, sems):
    pairs = ((upstream_hbm, upstream_ref), (up_hbm, up_ref))
    copies = [pltpu.make_async_copy(a, b, sems.at[i]) for i, (a, b) in enumerate(pairs)]
    for copy in copies:
        copy.start()
    for copy in copies:
        copy.wait()
    back_ref[...] = lax.dot_general(upstream_ref[...], up_ref[...], NT, preferred_element_type=F32)


def load_kernel(pieces, weight_hbm, at_hbm, new_hbm, after_ref, weight_ref, at_ref, new_ref, sems):
    size = weight_ref.shape[0] // 8 // pieces * 8
    starts = [i * size for i in range(pieces)] + [weight_ref.shape[0]]
    pairs = [(weight_hbm.at[a:b], weight_ref.at[a:b]) for a, b in zip(starts[:-1], starts[1:])]
    pairs += [(at_hbm, at_ref), (new_hbm, new_ref)]
    copies = [pltpu.make_async_copy(a, b, sems.at[i]) for i, (a, b) in enumerate(pairs)]
    for copy in copies:
        copy.start()
    for copy in copies:
        copy.wait()


def whole_rows(half, core, message, other):
    a, b = message[:, :half], other[:, :half]
    first = core == 0
    return jnp.concatenate([jnp.where(first, a, b), jnp.where(first, b, a)], axis=1)


def two_terms(value):
    high = value.astype(BF16).astype(F32)
    return jnp.concatenate([high, value - high], axis=1).astype(BF16)


def product_kernel(count, with_low, with_own, tokens, held_ref, at_ref, *refs):
    core = positions()[2]
    units, depth = held_ref.shape
    parts = [whole_rows(depth // 2, core, refs[i], refs[count + i]) for i in range(count)]
    refs = refs[2 * count :]
    if with_own:
        parts.append(refs[0][...])
        refs = refs[1:]
    rows = jnp.concatenate(parts, axis=0)
    lead = 0
    if with_low:
        low = lax.dot_general(rows, at_ref[...], NT, preferred_element_type=F32)
        lead = 2 * low.shape[1]
        refs[0][:, :lead] = two_terms(low)
    rows = rows.T
    for start in range(0, units, STEP):
        end = min(start + STEP, units)
        result = jnp.dot(held_ref[start:end], rows, preferred_element_type=F32).T
        for i, ref in enumerate(refs):
            ref[:, lead + start : lead + end] = result[i * tokens : (i + 1) * tokens].astype(ref.dtype)


def coef_kernel(groups, half, near, at_ref, new_ref, own_table, own_hidden, *rest):
    messages, others = rest[: groups - 1], rest[groups - 1 : groups - 1 + near]
    outs = rest[groups - 1 + near :]
    lows, coef_ref, loss_ref = outs[: near + 1], outs[near + 1], outs[near + 2]
    own, _, core = positions()
    tokens = own_hidden.shape[0]
    rows = [own_hidden[...]] + [whole_rows(half, core, messages[i], others[i]) for i in range(near)]
    low = lax.dot_general(jnp.concatenate(rows, axis=0), at_ref[...], NT, preferred_element_type=F32)
    for i, ref in enumerate(lows):
        ref[...] = low[i * tokens : (i + 1) * tokens]
    tables = [own_table[...]]
    for message in messages:
        terms = message[: 4 * BLOCK, half:].astype(F32)
        tables.append(terms[:BLOCK] + terms[BLOCK : 2 * BLOCK] + terms[2 * BLOCK : 3 * BLOCK])
    ordered = []
    for j in range(groups):
        table = tables[0]
        for d in range(1, groups):
            table = jnp.where((own ^ j) == d, tables[d], table)
        ordered.append(table)
    length = new_ref.shape[2]
    place = lax.broadcasted_iota(jnp.int32, (1, LANES), 1)
    diagonal = lax.broadcasted_iota(jnp.int32, (length, LANES), 0) == lax.broadcasted_iota(jnp.int32, (length, LANES), 1)
    new = new_ref[0]
    new = jnp.concatenate([new, jnp.zeros((groups, LANES - length), F32)], axis=1)
    together = COMP // groups
    parts = []
    loss = jnp.zeros((1, LANES), F32)
    for j in range(groups):
        prompt = ordered[j // together * together : (j // together + 1) * together]
        mean = sum(table[3:4] for table in prompt) / COMP
        square = sum(table[4:5] for table in prompt) / COMP
        spread = jnp.sqrt(jnp.maximum(square - mean * mean, SPREAD_FLOOR))
        old, reward, count = ordered[j][0:1], ordered[j][1:2], ordered[j][2:3]
        advantage = (reward - mean) / spread
        ratio = jnp.exp(new[j : j + 1] - old)
        live = (place.astype(F32) < count) & (place < length)
        coef = jnp.where(live, -(advantage * ratio) / (count * COMP), 0.0)
        loss = loss + coef
        column = jnp.sum(jnp.where(diagonal, coef, 0.0), axis=1, keepdims=True)
        parts.append(jnp.broadcast_to(column, (length, LANES)))
    coef_ref[...] = jnp.concatenate(parts, axis=0)
    loss_ref[...] = jnp.sum(loss, axis=1, keepdims=True)


def adapter_kernel(groups, share, ride_rows, *refs):
    lows, (far, back_ref, other_ref, coef_ref, upstream_ref) = refs[: groups - 1], refs[groups - 1 : groups + 4]
    messages, (own_term, own_back, low_ref, term) = refs[groups + 4 : 2 * groups + 3], refs[2 * groups + 3 :]
    own = positions()[0]
    coef = coef_ref[:, 0:1]
    rank = term.shape[0]
    low = far[:, :rank].astype(F32) + far[:, rank : 2 * rank].astype(F32)
    for ref in lows:
        low = low + ref[...]
    low = low.astype(BF16)
    low_ref[...] = low
    gradient = (coef * upstream_ref[...].astype(F32)).astype(BF16)
    term[...] = ADAPTER_SCALING * lax.dot_general(low, gradient, TN, preferred_element_type=F32)
    back = coef * (back_ref[...] + other_ref[...])
    own_back[...] = back.astype(BF16)
    stack = back.shape[0] // ride_rows
    ride = jnp.concatenate([back[i * ride_rows : (i + 1) * ride_rows] for i in range(stack)], axis=1).astype(BF16)
    lanes = stack * rank
    for d in range(groups):
        if share % 8 == 0:
            piece = term[pl.ds(pl.multiple_of((own ^ d) * share, share), share), :]
        else:
            piece = term[:share]
            for j in range(1, groups):
                piece = jnp.where((own ^ d) == j, term[j * share : (j + 1) * share], piece)
        if d == 0:
            own_term[...] = piece
            continue
        if share < ride_rows:
            piece = jnp.concatenate([piece, jnp.zeros((ride_rows - share, piece.shape[1]), F32)], axis=0)
        messages[d - 1][:, :lanes] = ride
        messages[d - 1][:, lanes:] = piece.astype(BF16)


def output_kernel(lead, total_ref, low_ref, up_ref, far, *rest):
    total = total_ref[...] + ADAPTER_SCALING * jnp.dot(low_ref[...], up_ref[...], preferred_element_type=F32)
    total = total + far[:, lead:].astype(F32)
    for ref in rest[:-1]:
        total = total + ref[...].astype(F32)
    rest[-1][...] = total.astype(BF16)


def gradient_kernel(groups, rank, share, ride_rows, own_term, own_back, own_hidden, *rest):
    arrived, messages, others = (rest[i * (groups - 1) : (i + 1) * (groups - 1)] for i in range(3))
    up_ref, down_ref = rest[3 * (groups - 1) :]
    core = positions()[2]
    half = own_hidden.shape[1] // 2
    tokens = own_hidden.shape[0]
    stack = tokens // ride_rows
    lanes = stack * rank
    hidden = [own_hidden[...]]
    backs = [own_back[...].astype(F32)]
    total = own_term[...]
    for come, message, other in zip(arrived, messages, others):
        total = total + come[:, lanes:].astype(F32)[:share]
        ride = come[:, :lanes].astype(F32)
        backs += [ride[:, i * rank : (i + 1) * rank] for i in range(stack)]
        hidden.append(whole_rows(half, core, message, other))
    up_ref[...] = total
    back = jnp.concatenate(backs, axis=0).astype(BF16)
    hidden = jnp.concatenate(hidden, axis=0)
    down_ref[...] = ADAPTER_SCALING * lax.dot_general(back, hidden, TN, preferred_element_type=F32)


def on_device(
    hidden_input_slots,
    base_weight,
    adapter_a,
    adapter_up_matrix,
    upstream,
    logp_new,
    logp_old,
    rewards,
    comp_lengths,
    assignment,
):
    groups = lax.axis_size("group")
    tokens = hidden_input_slots.shape[0]
    depth, units = base_weight.shape
    half = depth // 2
    rank = adapter_a.shape[1]
    others = range(1, groups)
    at, weight = adapter_a.T, base_weight.T

    *messages, own_table, own_hidden = call(
        functools.partial(pack_kernel, groups, depth),
        "pack",
        [pltpu.VMEM((tokens, half + LANES), BF16)] * (groups - 1)
        + [pltpu.VMEM((BLOCK, LANES), F32), pltpu.VMEM((tokens, depth), BF16)],
        [HBM] * 5,
        scratch=[
            pltpu.VMEM(logp_old.shape, F32),
            pltpu.SMEM(rewards.shape, F32),
            pltpu.SMEM(comp_lengths.shape, jnp.int32),
            pltpu.SMEM(assignment.shape, jnp.int32),
            pltpu.SemaphoreType.DMA((groups,)),
            pltpu.SemaphoreType.DMA((4,)),
        ],
        moved=2 * units * depth,
    )(*map(in_hbm, (hidden_input_slots, logp_old, rewards, comp_lengths, assignment)))
    got = {d: swap(messages[d - 1], "group", d) for d in reversed(others)}
    upstream, up, back = call(
        back_kernel,
        "back",
        [pltpu.VMEM((tokens, units), BF16), pltpu.VMEM((rank, units), BF16), pltpu.VMEM((tokens, rank), F32)],
        [HBM] * 2,
        scratch=[pltpu.SemaphoreType.DMA((2,))],
    )(*map(in_hbm, (upstream, adapter_up_matrix)))
    weight, at, new = call(
        functools.partial(load_kernel, 8),
        "load",
        [pltpu.VMEM((units, depth), BF16), pltpu.VMEM((rank, depth), BF16), pltpu.VMEM(logp_new.shape, F32)],
        [HBM] * 3 + [ANY],
        scratch=[pltpu.SemaphoreType.DMA((10,))],
    )(*map(in_hbm, (weight, at, logp_new)), back)
    weight, back, got = lax.optimization_barrier((weight, back, got))
    back = sum_over_pairs(back)
    theirs = {d: swap(got[d], "fsdp", 1) for d in reversed(others)}

    far, near = groups - 1, list(range(1, groups - 1))
    lead = 2 * rank
    came = {}
    (result,) = call(
        functools.partial(product_kernel, 1, True, False, tokens),
        "product",
        [pltpu.VMEM((tokens, lead + units), BF16)],
        [VMEM] * 4,
        flops=2 * units * tokens * depth,
        moved=units * depth * 2,
    )(weight, at, got[far], theirs[far])
    came[far] = swap(result, "group", far)
    *lows, coef, loss = call(
        functools.partial(coef_kernel, groups, half, len(near)),
        "coef",
        [pltpu.VMEM((tokens, rank), F32)] * (len(near) + 1)
        + [pltpu.VMEM((tokens, LANES), F32), jax.ShapeDtypeStruct((1, 1), F32)],
        [VMEM] * (3 + groups + len(near)),
    )(at, new, own_table, own_hidden, *[got[d] for d in others], *[theirs[d] for d in near])
    low_terms = [lows[0]] + [swap(low, "group", d) for d, low in zip(near, lows[1:])]
    *results, kept = call(
        functools.partial(product_kernel, len(near), False, True, tokens),
        "product",
        [pltpu.VMEM((tokens, units), BF16)] * len(near) + [pltpu.VMEM((tokens, units), F32)],
        [VMEM] * (3 + 2 * len(near)),
        flops=2 * units * tokens * depth * groups,
        moved=units * depth * 2,
    )(weight, at, *[got[d] for d in near], *[theirs[d] for d in near], own_hidden)
    for d, result in zip(near, results):
        came[d] = swap(result, "group", d)

    share = rank // groups
    ride_rows = max(share, 16)
    lanes = tokens // ride_rows * rank
    *pieces, own_term, own_back, low = call(
        functools.partial(adapter_kernel, groups, share, ride_rows),
        "adapter",
        [pltpu.VMEM((ride_rows, lanes + units), BF16)] * (groups - 1)
        + [pltpu.VMEM((share, units), F32), pltpu.VMEM((tokens, rank), BF16), pltpu.VMEM((tokens, rank), BF16)],
        [VMEM] * (groups + 4),
        scratch=[pltpu.VMEM((rank, units), F32)],
    )(*low_terms, came[far], back, swap(back, "fsdp", 1), coef, upstream)
    arrived = {d: swap(pieces[d - 1], "group", d) for d in reversed(others)}
    (projection_output,) = call(
        functools.partial(output_kernel, lead),
        "output",
        [jax.ShapeDtypeStruct((tokens, units), BF16)],
        [VMEM] * (4 + len(near)),
    )(kept, low, up, came[far], *[came[d] for d in near])
    gradient_up, gradient_down = call(
        functools.partial(gradient_kernel, groups, rank, share, ride_rows),
        "gradient",
        [jax.ShapeDtypeStruct((share, units), F32), jax.ShapeDtypeStruct((rank, depth), F32)],
        [VMEM] * (3 * groups),
    )(
        own_term,
        own_back,
        own_hidden,
        *[arrived[d] for d in others],
        *[got[d] for d in others],
        *[theirs[d] for d in others],
    )
    return (projection_output, gradient_down.T, gradient_up, loss[0])


def solution(mesh):
    return jax.shard_map(
        on_device,
        mesh=mesh,
        in_specs=(
            P("group", None),
            P("group", "fsdp"),
            P("group", None),
            P(None, "fsdp"),
            P("group", "fsdp"),
            P("group", None, None),
            P("group", None, None),
            P("group", None),
            P("group", None),
            P("group", None),
        ),
        out_specs=(P("group", "fsdp"), P("group", None), P("group", "fsdp"), P("group")),
        check_vma=False,
    )
```

```python
import functools

import jax
import jax.numpy as jnp
from jax import lax
from jax.experimental import pallas as pl
from jax.experimental.pallas import tpu as pltpu
from jax.sharding import PartitionSpec as P

COMP = 16


ADAPTER_SCALING = 0.25
SPREAD_FLOOR = 0.16
F32 = jnp.float32
BF16 = jnp.bfloat16
LANES = 128
BLOCK = 8
PEAK_FLOPS, PEAK_BYTES = 1.15e9, 3.6e6
STEP = 512
NT = (((1,), (1,)), ((), ()))
TN = (((0,), (0,)), ((), ()))
VMEM = pl.BlockSpec(memory_space=pltpu.VMEM)
SMEM = pl.BlockSpec(memory_space=pltpu.SMEM)
HBM = pl.BlockSpec(memory_space=pltpu.HBM)
ANY = pl.BlockSpec(memory_space=pl.ANY)


def swap(array, axis, distance):
    size = lax.axis_size(axis)
    return lax.ppermute(array, axis, [(i, i ^ distance) for i in range(size)])


def halves_over_fsdp(partial):
    size = lax.axis_size("fsdp")
    if size & (size - 1):
        total = lax.psum(partial, "fsdp")
        return total, jnp.zeros_like(total)
    distance = 1
    while distance < size // 2:
        partial = partial + swap(partial, "fsdp", distance)
        distance *= 2
    return partial, swap(partial, "fsdp", distance)


def after(array, earlier):
    return lax.optimization_barrier((array, earlier))[0]


def call(body, name, cost, outs, ins, scratch=()):
    return pl.pallas_call(
        body,
        out_shape=outs,
        in_specs=ins,
        out_specs=[VMEM] * len(outs),
        scratch_shapes=scratch,
        compiler_params=pltpu.CompilerParams(vmem_limit_bytes=8 << 20),
        cost_estimate=pl.CostEstimate(
            flops=int(cost * PEAK_FLOPS), bytes_accessed=int(cost * PEAK_BYTES), transcendentals=0
        ),
        name=name,
    )


def in_hbm(array):
    return pltpu.with_memory_space_constraint(array, pltpu.HBM)


def positions():
    own, member = lax.axis_index("group"), lax.axis_index("fsdp")
    return own, member, lax.rem(member, 2)


def start_all(pairs, sems, first=0):
    copies = [pltpu.make_async_copy(a, b, sems.at[first + i]) for i, (a, b) in enumerate(pairs)]
    for copy in copies:
        copy.start()
    return copies


def pack_kernel(groups, depth, hidden_ref, old_hbm, reward_hbm, length_hbm, dest_hbm, new_hbm, at_hbm, upstream_hbm, up_hbm, *rest):
    messages, own_table, own_hidden = rest[: groups - 1], rest[groups - 1], rest[groups]
    new_ref, at_ref, upstream_ref, up_ref, back_ref = rest[groups + 1 : groups + 6]
    old_ref, reward_ref, length_ref, dest_ref, sems, small_sems = rest[groups + 6 :]
    own, _, core = positions()
    half = depth // 2
    small = start_all(
        [(old_hbm, old_ref), (reward_hbm, reward_ref), (length_hbm, length_ref), (dest_hbm, dest_ref)], small_sems
    )
    small += start_all([(upstream_hbm, upstream_ref), (up_hbm, up_ref)], small_sems, 4)
    pairs = []
    for d in reversed(range(1, groups)):
        start = pl.multiple_of((own ^ d) * depth + core * half, LANES)
        pairs.append((hidden_ref.at[:, pl.ds(start, half)], messages[d - 1].at[:, :half]))
    pairs.append((hidden_ref.at[:, pl.ds(pl.multiple_of(own * depth, LANES), depth)], own_hidden))
    copies = start_all(pairs + [(new_hbm, new_ref), (at_hbm, at_ref)], sems)
    for copy in small:
        copy.wait()
    total, squares = jnp.float32(0), jnp.float32(0)
    for k in range(groups):
        total += reward_ref[0, k]
        squares += reward_ref[0, k] * reward_ref[0, k]
    old = old_ref[0]
    old = jnp.concatenate([old, jnp.zeros((groups, LANES - old.shape[1]), F32)], axis=1)
    for d in range(groups):
        line, reward, length = jnp.zeros((1, LANES), F32), jnp.float32(0), jnp.float32(0)
        for k in range(groups):
            chosen = dest_ref[0, k] == (own ^ d)
            line = jnp.where(chosen, old[k : k + 1], line)
            reward = jnp.where(chosen, reward_ref[0, k], reward)
            length = jnp.where(chosen, length_ref[0, k].astype(F32), length)
        lines = [line] + [jnp.full((1, LANES), x, F32) for x in (reward, length, total, squares)]
        value = jnp.concatenate(lines + [jnp.zeros((BLOCK - len(lines), LANES), F32)], axis=0)
        if d == 0:
            own_table[...] = value
            continue
        terms = []
        for _ in range(3):
            terms.append(value.astype(BF16).astype(F32))
            value = value - terms[-1]
        terms = jnp.concatenate(terms + [jnp.zeros((BLOCK, LANES), F32)], axis=0)
        messages[d - 1][: 4 * BLOCK, half:] = terms.astype(BF16)
    back_ref[...] = lax.dot_general(upstream_ref[...], up_ref[...], NT, preferred_element_type=F32)
    for copy in copies:
        copy.wait()


def whole_rows(half, core, message, other):
    a, b = message[:, :half], other[:, :half]
    first = core == 0
    return jnp.concatenate([jnp.where(first, a, b), jnp.where(first, b, a)], axis=1)


def two_terms(value):
    high = value.astype(BF16).astype(F32)
    return jnp.concatenate([high, value - high], axis=1).astype(BF16)


def far_kernel(held_ref, at_ref, message, other, result_ref):
    units, depth = held_ref.shape
    rows = whole_rows(depth // 2, positions()[2], message, other)
    low = lax.dot_general(rows, at_ref[...], NT, preferred_element_type=F32)
    lead = 2 * low.shape[1]
    result_ref[:, :lead] = two_terms(low)
    rows = rows.T
    for start in range(0, units, STEP):
        end = min(start + STEP, units)
        result = jnp.dot(held_ref[start:end], rows, preferred_element_type=F32).T
        result_ref[:, lead + start : lead + end] = result.astype(BF16)


def near_kernel(count, tokens, held_ref, early, later, *refs):
    units, depth = held_ref.shape
    core = positions()[2]
    parts = [whole_rows(depth // 2, core, refs[i], refs[count + i]) for i in range(count)] + [refs[2 * count][...]]
    rows = jnp.concatenate(parts, axis=0).T
    for start in range(0, units, STEP):
        end = min(start + STEP, units)
        result = jnp.dot(held_ref[start:end], rows, preferred_element_type=F32).T
        for i, ref in enumerate(refs[2 * count + 1 :]):
            ref[:, start:end] = result[i * tokens : (i + 1) * tokens].astype(ref.dtype)


def coef_kernel(groups, half, near, earlier, at_ref, new_ref, own_table, own_hidden, *rest):
    messages, others = rest[: groups - 1], rest[groups - 1 : groups - 1 + near]
    outs = rest[groups - 1 + near :]
    lows, coef_ref, loss_ref = outs[: near + 1], outs[near + 1], outs[near + 2]
    own, _, core = positions()
    tokens = own_hidden.shape[0]
    rows = [own_hidden[...]] + [whole_rows(half, core, messages[i], others[i]) for i in range(near)]
    low = lax.dot_general(jnp.concatenate(rows, axis=0), at_ref[...], NT, preferred_element_type=F32)
    for i, ref in enumerate(lows):
        ref[...] = low[i * tokens : (i + 1) * tokens]
    tables = [own_table[...]]
    for message in messages:
        terms = message[: 4 * BLOCK, half:].astype(F32)
        tables.append(terms[:BLOCK] + terms[BLOCK : 2 * BLOCK] + terms[2 * BLOCK : 3 * BLOCK])
    ordered = []
    for j in range(groups):
        table = tables[0]
        for d in range(1, groups):
            table = jnp.where((own ^ j) == d, tables[d], table)
        ordered.append(table)
    length = new_ref.shape[2]
    place = lax.broadcasted_iota(jnp.int32, (1, LANES), 1)
    diagonal = lax.broadcasted_iota(jnp.int32, (length, LANES), 0) == lax.broadcasted_iota(jnp.int32, (length, LANES), 1)
    new = new_ref[0]
    new = jnp.concatenate([new, jnp.zeros((groups, LANES - length), F32)], axis=1)
    together = COMP // groups
    parts = []
    loss = jnp.zeros((1, LANES), F32)
    for j in range(groups):
        prompt = ordered[j // together * together : (j // together + 1) * together]
        mean = sum(table[3:4] for table in prompt) / COMP
        square = sum(table[4:5] for table in prompt) / COMP
        spread = jnp.sqrt(jnp.maximum(square - mean * mean, SPREAD_FLOOR))
        old, reward, count = ordered[j][0:1], ordered[j][1:2], ordered[j][2:3]
        advantage = (reward - mean) / spread
        ratio = jnp.exp(new[j : j + 1] - old)
        live = (place.astype(F32) < count) & (place < length)
        coef = jnp.where(live, -(advantage * ratio) / (count * COMP), 0.0)
        loss = loss + coef
        column = jnp.sum(jnp.where(diagonal, coef, 0.0), axis=1, keepdims=True)
        parts.append(jnp.broadcast_to(column, (length, LANES)))
    coef_ref[...] = jnp.concatenate(parts, axis=0)
    loss_ref[...] = jnp.sum(loss, axis=1, keepdims=True)


def adapter_kernel(groups, share, ride_rows, *refs):
    lows, (far, back_ref, other_ref, coef_ref, upstream_ref) = refs[: groups - 1], refs[groups - 1 : groups + 4]
    messages, (own_term, own_back, low_ref, term) = refs[groups + 4 : 2 * groups + 3], refs[2 * groups + 3 :]
    own = positions()[0]
    coef = coef_ref[:, 0:1]
    rank = term.shape[0]
    low = far[:, :rank].astype(F32) + far[:, rank : 2 * rank].astype(F32)
    for ref in lows:
        low = low + ref[...]
    low = low.astype(BF16)
    low_ref[...] = low
    gradient = (coef * upstream_ref[...].astype(F32)).astype(BF16)
    term[...] = ADAPTER_SCALING * lax.dot_general(low, gradient, TN, preferred_element_type=F32)
    back = coef * (back_ref[...] + other_ref[...])
    own_back[...] = back.astype(BF16)
    stack = back.shape[0] // ride_rows
    ride = jnp.concatenate([back[i * ride_rows : (i + 1) * ride_rows] for i in range(stack)], axis=1).astype(BF16)
    lanes = stack * rank
    for d in range(groups):
        if share % 8 == 0:
            piece = term[pl.ds(pl.multiple_of((own ^ d) * share, share), share), :]
        else:
            piece = term[:share]
            for j in range(1, groups):
                piece = jnp.where((own ^ d) == j, term[j * share : (j + 1) * share], piece)
        if d == 0:
            own_term[...] = piece
            continue
        if share < ride_rows:
            piece = jnp.concatenate([piece, jnp.zeros((ride_rows - share, piece.shape[1]), F32)], axis=0)
        messages[d - 1][:, :lanes] = ride
        messages[d - 1][:, lanes:] = piece.astype(BF16)


def output_kernel(lead, total_ref, low_ref, up_ref, far, *rest):
    total = total_ref[...] + ADAPTER_SCALING * jnp.dot(low_ref[...], up_ref[...], preferred_element_type=F32)
    total = total + far[:, lead:].astype(F32)
    for ref in rest[:-1]:
        total = total + ref[...].astype(F32)
    rest[-1][...] = total.astype(BF16)


def gradient_kernel(groups, rank, share, ride_rows, own_term, own_back, own_hidden, *rest):
    arrived, messages, others = (rest[i * (groups - 1) : (i + 1) * (groups - 1)] for i in range(3))
    up_ref, down_ref = rest[3 * (groups - 1) :]
    core = positions()[2]
    half = own_hidden.shape[1] // 2
    tokens = own_hidden.shape[0]
    stack = tokens // ride_rows
    lanes = stack * rank
    hidden = [own_hidden[...]]
    backs = [own_back[...].astype(F32)]
    total = own_term[...]
    for come, message, other in zip(arrived, messages, others):
        total = total + come[:, lanes:].astype(F32)[:share]
        ride = come[:, :lanes].astype(F32)
        backs += [ride[:, i * rank : (i + 1) * rank] for i in range(stack)]
        hidden.append(whole_rows(half, core, message, other))
    up_ref[...] = total
    back = jnp.concatenate(backs, axis=0).astype(BF16)
    hidden = jnp.concatenate(hidden, axis=0)
    down_ref[...] = ADAPTER_SCALING * lax.dot_general(back, hidden, TN, preferred_element_type=F32)


def on_device(
    hidden_input_slots,
    base_weight,
    adapter_a,
    adapter_up_matrix,
    upstream,
    logp_new,
    logp_old,
    rewards,
    comp_lengths,
    assignment,
):
    groups = lax.axis_size("group")
    tokens = hidden_input_slots.shape[0]
    depth, units = base_weight.shape
    half = depth // 2
    rank = adapter_a.shape[1]
    others = range(1, groups)
    at, weight = adapter_a.T, base_weight.T

    *messages, own_table, own_hidden, new, at, upstream, up, back = call(
        functools.partial(pack_kernel, groups, depth),
        "pack",
        1.8,
        [pltpu.VMEM((tokens, half + LANES), BF16)] * (groups - 1)
        + [
            pltpu.VMEM((BLOCK, LANES), F32),
            pltpu.VMEM((tokens, depth), BF16),
            pltpu.VMEM(logp_new.shape, F32),
            pltpu.VMEM((rank, depth), BF16),
            pltpu.VMEM((tokens, units), BF16),
            pltpu.VMEM((rank, units), BF16),
            pltpu.VMEM((tokens, rank), F32),
        ],
        [HBM] * 9,
        scratch=[
            pltpu.VMEM(logp_old.shape, F32),
            pltpu.SMEM(rewards.shape, F32),
            pltpu.SMEM(comp_lengths.shape, jnp.int32),
            pltpu.SMEM(assignment.shape, jnp.int32),
            pltpu.SemaphoreType.DMA((groups + 2,)),
            pltpu.SemaphoreType.DMA((6,)),
        ],
    )(
        *map(
            in_hbm,
            (
                hidden_input_slots,
                logp_old,
                rewards,
                comp_lengths,
                assignment,
                logp_new,
                at,
                upstream,
                adapter_up_matrix,
            ),
        )
    )
    got = {d: swap(messages[d - 1], "group", d) for d in reversed(others)}
    held = pltpu.with_memory_space_constraint(weight, pltpu.VMEM)
    far, near = groups - 1, list(range(1, groups - 1))
    early, last = halves_over_fsdp(back)
    theirs = {far: swap(after(got[far], early), "fsdp", 1)}

    lead = 2 * rank
    came = {}
    (result,) = call(far_kernel, "far", 2.3, [pltpu.VMEM((tokens, lead + units), BF16)], [VMEM] * 4)(
        held, at, got[far], theirs[far]
    )
    came[far] = swap(result, "group", far)
    for d in near:
        theirs[d] = swap(got[d], "fsdp", 1)
    *lows, coef, loss = call(
        functools.partial(coef_kernel, groups, half, len(near)),
        "coef",
        0.8,
        [pltpu.VMEM((tokens, rank), F32)] * (len(near) + 1)
        + [pltpu.VMEM((tokens, LANES), F32), jax.ShapeDtypeStruct((1, 1), F32)],
        [ANY] + [VMEM] * (3 + groups + len(near)),
    )(result, at, new, own_table, own_hidden, *[got[d] for d in others], *[theirs[d] for d in near])
    low_terms = [lows[0]] + [swap(low, "group", d) for d, low in zip(near, lows[1:])]
    *results, kept = call(
        functools.partial(near_kernel, len(near), tokens),
        "near",
        2.4,
        [pltpu.VMEM((tokens, units), BF16)] * len(near) + [pltpu.VMEM((tokens, units), F32)],
        [VMEM, ANY, ANY] + [VMEM] * (1 + 2 * len(near)),
    )(held, last, coef, *[got[d] for d in near], *[theirs[d] for d in near], own_hidden)
    for d, result in zip(near, results):
        came[d] = swap(result, "group", d)

    share = rank // groups
    ride_rows = max(share, 16)
    lanes = tokens // ride_rows * rank
    *pieces, own_term, own_back, low = call(
        functools.partial(adapter_kernel, groups, share, ride_rows),
        "adapter",
        4.0,
        [pltpu.VMEM((ride_rows, lanes + units), BF16)] * (groups - 1)
        + [pltpu.VMEM((share, units), F32), pltpu.VMEM((tokens, rank), BF16), pltpu.VMEM((tokens, rank), BF16)],
        [VMEM] * (groups + 4),
        scratch=[pltpu.VMEM((rank, units), F32)],
    )(*low_terms, came[far], early, last, coef, upstream)
    arrived = {d: swap(pieces[d - 1], "group", d) for d in reversed(others)}
    (projection_output,) = call(
        functools.partial(output_kernel, lead),
        "output",
        1.0,
        [jax.ShapeDtypeStruct((tokens, units), BF16)],
        [VMEM] * (4 + len(near)),
    )(kept, low, up, came[far], *[came[d] for d in near])
    gradient_up, gradient_down = call(
        functools.partial(gradient_kernel, groups, rank, share, ride_rows),
        "gradient",
        1.2,
        [jax.ShapeDtypeStruct((share, units), F32), jax.ShapeDtypeStruct((rank, depth), F32)],
        [VMEM] * (3 * groups),
    )(
        own_term,
        own_back,
        own_hidden,
        *[arrived[d] for d in others],
        *[got[d] for d in others],
        *[theirs[d] for d in others],
    )
    return (projection_output, gradient_down.T, gradient_up, loss[0])


def solution(mesh):
    return jax.shard_map(
        on_device,
        mesh=mesh,
        in_specs=(
            P("group", None),
            P("group", "fsdp"),
            P("group", None),
            P(None, "fsdp"),
            P("group", "fsdp"),
            P("group", None, None),
            P("group", None, None),
            P("group", None),
            P("group", None),
            P("group", None),
        ),
        out_specs=(P("group", "fsdp"), P("group", None), P("group", "fsdp"), P("group")),
        check_vma=False,
    )
```

```python
import functools

import jax
import jax.numpy as jnp
from jax import lax
from jax.experimental import pallas as pl
from jax.experimental.pallas import tpu as pltpu
from jax.sharding import PartitionSpec as P

COMP = 16


ADAPTER_SCALING = 0.25
SPREAD_FLOOR = 0.16
F32 = jnp.float32
BF16 = jnp.bfloat16
LANES = 128
BLOCK = 8
PEAK_FLOPS, PEAK_BYTES = 1.15e9, 3.6e6
STEP = 512
NT = (((1,), (1,)), ((), ()))
TN = (((0,), (0,)), ((), ()))
VMEM = pl.BlockSpec(memory_space=pltpu.VMEM)
SMEM = pl.BlockSpec(memory_space=pltpu.SMEM)
HBM = pl.BlockSpec(memory_space=pltpu.HBM)
ANY = pl.BlockSpec(memory_space=pl.ANY)


def swap(array, axis, distance):
    size = lax.axis_size(axis)
    return lax.ppermute(array, axis, [(i, i ^ distance) for i in range(size)])


def swap_cores(array, axis, partner):
    size = lax.axis_size(axis)
    return lax.ppermute(array, axis, [(i, i ^ partner[i % 2]) for i in range(size)])


def sum_over_fsdp(partial, earlier):
    size = lax.axis_size("fsdp")
    if size & (size - 1):
        return lax.psum(partial, "fsdp")
    chip = partial + swap(partial, "fsdp", 1)
    if size == 8:
        one = swap_cores(chip, "fsdp", (2, 4))
        chip = after(chip, earlier) + swap(chip, "fsdp", 6)
        return chip + (one + swap(after(one, earlier), "fsdp", 1))
    parts = [chip] + [swap(chip, "fsdp", d) for d in range(2, size, 2)]
    while len(parts) > 1:
        parts = [parts[i] + parts[i + 1] for i in range(0, len(parts), 2)]
    return parts[0]


def after(array, earlier):
    return lax.optimization_barrier((array, earlier))[0]


def call(body, name, cost, outs, ins, scratch=()):
    return pl.pallas_call(
        body,
        out_shape=outs,
        in_specs=ins,
        out_specs=[VMEM] * len(outs),
        scratch_shapes=scratch,
        compiler_params=pltpu.CompilerParams(vmem_limit_bytes=8 << 20),
        cost_estimate=pl.CostEstimate(
            flops=int(cost * PEAK_FLOPS), bytes_accessed=int(cost * PEAK_BYTES), transcendentals=0
        ),
        name=name,
    )


def in_hbm(array):
    return pltpu.with_memory_space_constraint(array, pltpu.HBM)


def positions():
    own, member = lax.axis_index("group"), lax.axis_index("fsdp")
    return own, member, lax.rem(member, 2)


def start_all(pairs, sems, first=0):
    copies = [pltpu.make_async_copy(a, b, sems.at[first + i]) for i, (a, b) in enumerate(pairs)]
    for copy in copies:
        copy.start()
    return copies


def pack_kernel(groups, depth, hidden_ref, old_hbm, reward_hbm, length_hbm, dest_hbm, new_hbm, at_hbm, upstream_hbm, up_hbm, *rest):
    messages, own_table, own_hidden = rest[: groups - 1], rest[groups - 1], rest[groups]
    new_ref, at_ref, upstream_ref, up_ref, back_ref = rest[groups + 1 : groups + 6]
    old_ref, reward_ref, length_ref, dest_ref, sems, small_sems = rest[groups + 6 :]
    own, _, core = positions()
    half = depth // 2
    small = start_all(
        [(old_hbm, old_ref), (reward_hbm, reward_ref), (length_hbm, length_ref), (dest_hbm, dest_ref)], small_sems
    )
    small += start_all([(upstream_hbm, upstream_ref), (up_hbm, up_ref)], small_sems, 4)
    pairs = []
    for d in reversed(range(1, groups)):
        start = pl.multiple_of((own ^ d) * depth + core * half, LANES)
        pairs.append((hidden_ref.at[:, pl.ds(start, half)], messages[d - 1].at[:, :half]))
    pairs.append((hidden_ref.at[:, pl.ds(pl.multiple_of(own * depth, LANES), depth)], own_hidden))
    copies = start_all(pairs + [(new_hbm, new_ref), (at_hbm, at_ref)], sems)
    for copy in small:
        copy.wait()
    total, squares = jnp.float32(0), jnp.float32(0)
    for k in range(groups):
        total += reward_ref[0, k]
        squares += reward_ref[0, k] * reward_ref[0, k]
    old = old_ref[0]
    old = jnp.concatenate([old, jnp.zeros((groups, LANES - old.shape[1]), F32)], axis=1)
    for d in range(groups):
        line, reward, length = jnp.zeros((1, LANES), F32), jnp.float32(0), jnp.float32(0)
        for k in range(groups):
            chosen = dest_ref[0, k] == (own ^ d)
            line = jnp.where(chosen, old[k : k + 1], line)
            reward = jnp.where(chosen, reward_ref[0, k], reward)
            length = jnp.where(chosen, length_ref[0, k].astype(F32), length)
        lines = [line] + [jnp.full((1, LANES), x, F32) for x in (reward, length, total, squares)]
        value = jnp.concatenate(lines + [jnp.zeros((BLOCK - len(lines), LANES), F32)], axis=0)
        if d == 0:
            own_table[...] = value
            continue
        terms = []
        for _ in range(3):
            terms.append(value.astype(BF16).astype(F32))
            value = value - terms[-1]
        terms = jnp.concatenate(terms + [jnp.zeros((BLOCK, LANES), F32)], axis=0)
        messages[d - 1][: 4 * BLOCK, half:] = terms.astype(BF16)
    back_ref[...] = lax.dot_general(upstream_ref[...], up_ref[...], NT, preferred_element_type=F32)
    for copy in copies:
        copy.wait()


def whole_rows(half, core, message, other):
    a, b = message[:, :half], other[:, :half]
    first = core == 0
    return jnp.concatenate([jnp.where(first, a, b), jnp.where(first, b, a)], axis=1)


def middle(units):
    return units // 2 // LANES * LANES


def product_kernel(groups, earlier, held_ref, at_ref, own_hidden, *refs):
    count = groups - 1
    messages, others, refs = refs[:count], refs[count : 2 * count], refs[2 * count :]
    first, second, kept, nears, lows = refs[0], refs[1], refs[2], refs[3 : groups + 1], refs[groups + 1 :]
    units, depth = held_ref.shape
    tokens = own_hidden.shape[0]
    core = positions()[2]
    parts = [own_hidden[...]] + [whole_rows(depth // 2, core, a, b) for a, b in zip(messages, others)]
    rows = jnp.concatenate(parts, axis=0)
    low = lax.dot_general(rows, at_ref[...], NT, preferred_element_type=F32)
    for i, ref in enumerate(lows):
        ref[...] = low[i * tokens : (i + 1) * tokens]
    rows = rows.T
    center = middle(units)
    for start, end in [(i, min(i + STEP, center)) for i in range(0, center, STEP)] + [
        (i, min(i + STEP, units)) for i in range(center, units, STEP)
    ]:
        result = jnp.dot(held_ref[start:end], rows, preferred_element_type=F32).T
        for i, ref in enumerate([kept, *nears]):
            ref[:, start:end] = result[i * tokens : (i + 1) * tokens]
        last = result[count * tokens :].astype(BF16)
        if end <= center:
            first[:, start:end] = last
        else:
            second[:, start - center : end - center] = last


def add_kernel(count, first, second, *refs):
    center = first.shape[1]
    for i, (ref, out) in enumerate(zip(refs[:count], refs[count:])):
        out[...] = ref[...].astype(BF16)
        if i == 0:
            out[:, center:] = (ref[:, center:] + second[...].astype(F32)).astype(BF16)
        if i == count - 1:
            out[:, :center] = (ref[:, :center] + first[...].astype(F32)).astype(BF16)


def coef_kernel(groups, half, new_ref, own_table, *rest):
    messages, (coef_ref, loss_ref) = rest[: groups - 1], rest[groups - 1 :]
    own = positions()[0]
    tables = [own_table[...]]
    for message in messages:
        terms = message[: 4 * BLOCK, half:].astype(F32)
        tables.append(terms[:BLOCK] + terms[BLOCK : 2 * BLOCK] + terms[2 * BLOCK : 3 * BLOCK])
    ordered = []
    for j in range(groups):
        table = tables[0]
        for d in range(1, groups):
            table = jnp.where((own ^ j) == d, tables[d], table)
        ordered.append(table)
    length = new_ref.shape[2]
    place = lax.broadcasted_iota(jnp.int32, (1, LANES), 1)
    diagonal = lax.broadcasted_iota(jnp.int32, (length, LANES), 0) == lax.broadcasted_iota(jnp.int32, (length, LANES), 1)
    new = new_ref[0]
    new = jnp.concatenate([new, jnp.zeros((groups, LANES - length), F32)], axis=1)
    together = COMP // groups
    parts = []
    loss = jnp.zeros((1, LANES), F32)
    for j in range(groups):
        prompt = ordered[j // together * together : (j // together + 1) * together]
        mean = sum(table[3:4] for table in prompt) / COMP
        square = sum(table[4:5] for table in prompt) / COMP
        spread = jnp.sqrt(jnp.maximum(square - mean * mean, SPREAD_FLOOR))
        old, reward, count = ordered[j][0:1], ordered[j][1:2], ordered[j][2:3]
        advantage = (reward - mean) / spread
        ratio = jnp.exp(new[j : j + 1] - old)
        live = (place.astype(F32) < count) & (place < length)
        coef = jnp.where(live, -(advantage * ratio) / (count * COMP), 0.0)
        loss = loss + coef
        column = jnp.sum(jnp.where(diagonal, coef, 0.0), axis=1, keepdims=True)
        parts.append(jnp.broadcast_to(column, (length, LANES)))
    coef_ref[...] = jnp.concatenate(parts, axis=0)
    loss_ref[...] = jnp.sum(loss, axis=1, keepdims=True)


def adapter_kernel(groups, share, ride_rows, *refs):
    lows, (back_ref, coef_ref, upstream_ref) = refs[:groups], refs[groups : groups + 3]
    messages, (own_term, own_back, low_ref, term) = refs[groups + 3 : 2 * groups + 2], refs[2 * groups + 2 :]
    own = positions()[0]
    coef = coef_ref[:, 0:1]
    rank = term.shape[0]
    low = lows[0][...]
    for ref in lows[1:]:
        low = low + ref[...]
    low = low.astype(BF16)
    low_ref[...] = low
    gradient = (coef * upstream_ref[...].astype(F32)).astype(BF16)
    term[...] = ADAPTER_SCALING * lax.dot_general(low, gradient, TN, preferred_element_type=F32)
    back = coef * back_ref[...]
    own_back[...] = back.astype(BF16)
    stack = back.shape[0] // ride_rows
    ride = jnp.concatenate([back[i * ride_rows : (i + 1) * ride_rows] for i in range(stack)], axis=1).astype(BF16)
    lanes = stack * rank
    for d in range(groups):
        if share % 8 == 0:
            piece = term[pl.ds(pl.multiple_of((own ^ d) * share, share), share), :]
        else:
            piece = term[:share]
            for j in range(1, groups):
                piece = jnp.where((own ^ d) == j, term[j * share : (j + 1) * share], piece)
        if d == 0:
            own_term[...] = piece
            continue
        if share < ride_rows:
            piece = jnp.concatenate([piece, jnp.zeros((ride_rows - share, piece.shape[1]), F32)], axis=0)
        messages[d - 1][:, :lanes] = ride
        messages[d - 1][:, lanes:] = piece.astype(BF16)


def output_kernel(total_ref, low_ref, up_ref, *rest):
    total = total_ref[...] + ADAPTER_SCALING * jnp.dot(low_ref[...], up_ref[...], preferred_element_type=F32)
    for ref in rest[:-2]:
        total = total + ref[...].astype(F32)
    rest[-2][...] = total.astype(BF16)
    rest[-1][...] = jnp.zeros_like(rest[-1])


def gradient_kernel(groups, rank, share, ride_rows, written, own_term, own_back, own_hidden, *rest):
    arrived, messages, others = (rest[i * (groups - 1) : (i + 1) * (groups - 1)] for i in range(3))
    up_ref, down_ref = rest[3 * (groups - 1) :]
    core = positions()[2]
    half = own_hidden.shape[1] // 2
    tokens = own_hidden.shape[0]
    stack = tokens // ride_rows
    lanes = stack * rank
    hidden = [own_hidden[...]]
    backs = [own_back[...].astype(F32)]
    total = own_term[...]
    for come, message, other in zip(arrived, messages, others):
        total = total + come[:, lanes:].astype(F32)[:share]
        ride = come[:, :lanes].astype(F32)
        backs += [ride[:, i * rank : (i + 1) * rank] for i in range(stack)]
        hidden.append(whole_rows(half, core, message, other))
    up_ref[...] = total
    back = jnp.concatenate(backs, axis=0).astype(BF16)
    hidden = jnp.concatenate(hidden, axis=0)
    down_ref[...] = ADAPTER_SCALING * lax.dot_general(back, hidden, TN, preferred_element_type=F32)


def on_device(
    hidden_input_slots,
    base_weight,
    adapter_a,
    adapter_up_matrix,
    upstream,
    logp_new,
    logp_old,
    rewards,
    comp_lengths,
    assignment,
):
    groups = lax.axis_size("group")
    tokens = hidden_input_slots.shape[0]
    depth, units = base_weight.shape
    half = depth // 2
    rank = adapter_a.shape[1]
    others = range(1, groups)
    at, weight = adapter_a.T, base_weight.T

    *messages, own_table, own_hidden, new, at, upstream, up, back = call(
        functools.partial(pack_kernel, groups, depth),
        "pack",
        1.8,
        [pltpu.VMEM((tokens, half + LANES), BF16)] * (groups - 1)
        + [
            pltpu.VMEM((BLOCK, LANES), F32),
            pltpu.VMEM((tokens, depth), BF16),
            pltpu.VMEM(logp_new.shape, F32),
            pltpu.VMEM((rank, depth), BF16),
            pltpu.VMEM((tokens, units), BF16),
            pltpu.VMEM((rank, units), BF16),
            pltpu.VMEM((tokens, rank), F32),
        ],
        [HBM] * 9,
        scratch=[
            pltpu.VMEM(logp_old.shape, F32),
            pltpu.SMEM(rewards.shape, F32),
            pltpu.SMEM(comp_lengths.shape, jnp.int32),
            pltpu.SMEM(assignment.shape, jnp.int32),
            pltpu.SemaphoreType.DMA((groups + 2,)),
            pltpu.SemaphoreType.DMA((6,)),
        ],
    )(
        *map(
            in_hbm,
            (
                hidden_input_slots,
                logp_old,
                rewards,
                comp_lengths,
                assignment,
                logp_new,
                at,
                upstream,
                adapter_up_matrix,
            ),
        )
    )
    got = {d: swap(messages[d - 1], "group", d) for d in reversed(others)}
    held = pltpu.with_memory_space_constraint(weight, pltpu.VMEM)
    far, near = groups - 1, list(range(1, groups - 1))
    coef, loss = call(
        functools.partial(coef_kernel, groups, half),
        "coef",
        1.5,
        [pltpu.VMEM((tokens, LANES), F32), jax.ShapeDtypeStruct((1, 1), F32)],
        [VMEM] * (groups + 1),
    )(new, own_table, *[got[d] for d in others])

    back = sum_over_fsdp(back, coef)
    theirs = {d: swap(got[d], "fsdp", 1) for d in reversed(others)}

    first, second, kept, *terms = call(
        functools.partial(product_kernel, groups),
        "product",
        3.0,
        [
            pltpu.VMEM((tokens, middle(units)), BF16),
            pltpu.VMEM((tokens, units - middle(units)), BF16),
            pltpu.VMEM((tokens, units), F32),
        ]
        + [pltpu.VMEM((tokens, units), F32)] * len(near)
        + [pltpu.VMEM((tokens, rank), F32)] * groups,
        [ANY] + [VMEM] * (1 + 2 * groups),
    )(coef, held, at, own_hidden, *[got[d] for d in others], *[theirs[d] for d in others])
    lows = terms[len(near) :]
    first, second = swap(first, "group", near[0]), swap(second, "group", near[-1])
    lows = [lows[0]] + [swap(lows[d], "group", d) for d in others]
    results = call(
        functools.partial(add_kernel, len(near)),
        "add",
        0.5,
        [pltpu.VMEM((tokens, units), BF16)] * len(near),
        [VMEM] * (2 + len(near)),
    )(first, second, *terms[: len(near)])
    came = [swap(result, "group", d) for d, result in zip(near, results)]
    share = rank // groups
    ride_rows = max(share, 16)
    lanes = tokens // ride_rows * rank
    *pieces, own_term, own_back, low = call(
        functools.partial(adapter_kernel, groups, share, ride_rows),
        "adapter",
        4.0,
        [pltpu.VMEM((ride_rows, lanes + units), BF16)] * (groups - 1)
        + [pltpu.VMEM((share, units), F32), pltpu.VMEM((tokens, rank), BF16), pltpu.VMEM((tokens, rank), BF16)],
        [VMEM] * (groups + 3),
        scratch=[pltpu.VMEM((rank, units), F32)],
    )(*lows, back, coef, upstream)
    arrived = {d: swap(pieces[d - 1], "group", d) for d in reversed(others)}
    projection_output, written = call(
        output_kernel,
        "output",
        1.0,
        [jax.ShapeDtypeStruct((tokens, units), BF16), pltpu.VMEM((8, LANES), F32)],
        [VMEM] * (3 + len(near)),
    )(kept, low, up, *came)
    gradient_up, gradient_down = call(
        functools.partial(gradient_kernel, groups, rank, share, ride_rows),
        "gradient",
        1.2,
        [jax.ShapeDtypeStruct((share, units), F32), jax.ShapeDtypeStruct((rank, depth), F32)],
        [ANY] + [VMEM] * (3 * groups),
    )(
        written,
        own_term,
        own_back,
        own_hidden,
        *[arrived[d] for d in others],
        *[got[d] for d in others],
        *[theirs[d] for d in others],
    )
    return (projection_output, gradient_down.T, gradient_up, loss[0])


def solution(mesh):
    return jax.shard_map(
        on_device,
        mesh=mesh,
        in_specs=(
            P("group", None),
            P("group", "fsdp"),
            P("group", None),
            P(None, "fsdp"),
            P("group", "fsdp"),
            P("group", None, None),
            P("group", None, None),
            P("group", None),
            P("group", None),
            P("group", None),
        ),
        out_specs=(P("group", "fsdp"), P("group", None), P("group", "fsdp"), P("group")),
        check_vma=False,
    )
```

```python
import functools

import jax
import jax.numpy as jnp
from jax import lax
from jax.experimental import pallas as pl
from jax.experimental.pallas import tpu as pltpu
from jax.sharding import PartitionSpec as P

COMP = 16


ADAPTER_SCALING = 0.25
SPREAD_FLOOR = 0.16
F32 = jnp.float32
BF16 = jnp.bfloat16
LANES = 128
BLOCK = 8
PEAK_FLOPS, PEAK_BYTES = 1.15e9, 3.6e6
STEP = 512
NT = (((1,), (1,)), ((), ()))
TN = (((0,), (0,)), ((), ()))
VMEM = pl.BlockSpec(memory_space=pltpu.VMEM)
SMEM = pl.BlockSpec(memory_space=pltpu.SMEM)
HBM = pl.BlockSpec(memory_space=pltpu.HBM)
ANY = pl.BlockSpec(memory_space=pl.ANY)


def swap(array, axis, distance):
    size = lax.axis_size(axis)
    return lax.ppermute(array, axis, [(i, i ^ distance) for i in range(size)])


def swap_cores(array, axis, partner):
    size = lax.axis_size(axis)
    return lax.ppermute(array, axis, [(i, i ^ partner[i % 2]) for i in range(size)])


def swap_pair(array, partner):
    groups, size = lax.axis_size("group"), lax.axis_size("fsdp")
    return lax.ppermute(
        array,
        ("group", "fsdp"),
        [(g * size + f, (g ^ partner[f % 2]) * size + f) for g in range(groups) for f in range(size)],
    )


def sum_over_fsdp(partial, earlier):
    size = lax.axis_size("fsdp")
    if size & (size - 1):
        return lax.psum(partial, "fsdp")
    chip = partial + swap(partial, "fsdp", 1)
    if size == 8:
        one = swap_cores(chip, "fsdp", (2, 4))
        chip = after(chip, earlier) + swap(chip, "fsdp", 6)
        return chip + (one + swap(after(one, earlier), "fsdp", 1))
    parts = [chip] + [swap(chip, "fsdp", d) for d in range(2, size, 2)]
    while len(parts) > 1:
        parts = [parts[i] + parts[i + 1] for i in range(0, len(parts), 2)]
    return parts[0]


def after(array, earlier):
    return lax.optimization_barrier((array, earlier))[0]


def call(body, name, cost, outs, ins, scratch=(), out_specs=None):
    return pl.pallas_call(
        body,
        out_shape=outs,
        in_specs=ins,
        out_specs=out_specs or [VMEM] * len(outs),
        scratch_shapes=scratch,
        compiler_params=pltpu.CompilerParams(vmem_limit_bytes=8 << 20),
        cost_estimate=pl.CostEstimate(
            flops=int(cost * PEAK_FLOPS), bytes_accessed=int(cost * PEAK_BYTES), transcendentals=0
        ),
        name=name,
    )


def in_hbm(array):
    return pltpu.with_memory_space_constraint(array, pltpu.HBM)


def positions():
    own, member = lax.axis_index("group"), lax.axis_index("fsdp")
    return own, member, lax.rem(member, 2)


def start_all(pairs, sems, first=0):
    copies = [pltpu.make_async_copy(a, b, sems.at[first + i]) for i, (a, b) in enumerate(pairs)]
    for copy in copies:
        copy.start()
    return copies


def pack_kernel(groups, depth, hidden_ref, old_hbm, reward_hbm, length_hbm, dest_hbm, new_hbm, at_hbm, upstream_hbm, up_hbm, *rest):
    messages, table_ref, own_hidden = rest[: groups - 1], rest[groups - 1], rest[groups]
    new_ref, at_ref, upstream_ref, up_ref, back_ref = rest[groups + 1 : groups + 6]
    old_ref, reward_ref, length_ref, dest_ref, sems, small_sems = rest[groups + 6 :]
    own, _, core = positions()
    half = depth // 2
    small = start_all(
        [(old_hbm, old_ref), (reward_hbm, reward_ref), (length_hbm, length_ref), (dest_hbm, dest_ref)], small_sems
    )
    small += start_all([(upstream_hbm, upstream_ref), (up_hbm, up_ref)], small_sems, 4)
    pairs = []
    for d in reversed(range(1, groups)):
        start = pl.multiple_of((own ^ d) * depth + core * half, LANES)
        pairs.append((hidden_ref.at[:, pl.ds(start, half)], messages[d - 1]))
    pairs.append((hidden_ref.at[:, pl.ds(pl.multiple_of(own * depth, LANES), depth)], own_hidden))
    copies = start_all(pairs + [(new_hbm, new_ref), (at_hbm, at_ref)], sems)
    for copy in small:
        copy.wait()
    total, squares = jnp.float32(0), jnp.float32(0)
    for k in range(groups):
        total += reward_ref[0, k]
        squares += reward_ref[0, k] * reward_ref[0, k]
    old = old_ref[0]
    old = jnp.concatenate([old, jnp.zeros((groups, LANES - old.shape[1]), F32)], axis=1)
    for d in range(groups):
        line, reward, length = jnp.zeros((1, LANES), F32), jnp.float32(0), jnp.float32(0)
        for k in range(groups):
            chosen = dest_ref[0, k] == (own ^ d)
            line = jnp.where(chosen, old[k : k + 1], line)
            reward = jnp.where(chosen, reward_ref[0, k], reward)
            length = jnp.where(chosen, length_ref[0, k].astype(F32), length)
        lines = [line] + [jnp.full((1, LANES), x, F32) for x in (reward, length, total, squares)]
        table_ref[d * BLOCK : (d + 1) * BLOCK] = jnp.concatenate(
            lines + [jnp.zeros((BLOCK - len(lines), LANES), F32)], axis=0
        )
    back_ref[...] = lax.dot_general(upstream_ref[...], up_ref[...], NT, preferred_element_type=F32)
    for copy in copies:
        copy.wait()


def whole_rows(half, core, message, other):
    a, b = message[:, :half], other[:, :half]
    first = core == 0
    return jnp.concatenate([jnp.where(first, a, b), jnp.where(first, b, a)], axis=1)


def first_kernel(held_ref, at_ref, own_hidden, *refs):
    *messages, sums_ref, low_ref = refs
    messages = messages[::-1]
    units, depth = held_ref.shape
    half = depth // 2
    mine = pl.ds(pl.multiple_of(positions()[2] * half, LANES), half)
    rows = jnp.concatenate([own_hidden[:, mine]] + [ref[...] for ref in messages], axis=0)
    low_ref[...] = lax.dot_general(rows, at_ref[:, mine], NT, preferred_element_type=F32)
    rows = rows.T
    for start in range(0, units, STEP):
        end = min(start + STEP, units)
        sums_ref[start:end] = jnp.dot(held_ref[start:end, mine], rows, preferred_element_type=F32)


def second_kernel(groups, held_ref, at_ref, own_hidden, table_ref, sums_ref, low_ref, *refs):
    count = groups - 1
    others, refs = refs[:count][::-1], refs[count:]
    far, early, late, kept, nears, lows = *refs[:4], refs[4 : groups], refs[groups:]
    units, depth = held_ref.shape
    tokens, rank = own_hidden.shape[0], low_ref.shape[1]
    half = depth // 2
    core = positions()[2]
    rest = pl.ds(pl.multiple_of((1 - core) * half, LANES), half)
    rows = jnp.concatenate([own_hidden[:, rest]] + [ref[...] for ref in others], axis=0)
    low = low_ref[...] + lax.dot_general(rows, at_ref[:, rest], NT, preferred_element_type=F32)
    for i, ref in enumerate(lows):
        ref[:tokens] = low[i * tokens : (i + 1) * tokens]
        ref[tokens:] = table_ref[i * BLOCK : (i + 1) * BLOCK, :rank]
    rows = rows.T
    for start in range(0, units, STEP):
        end = min(start + STEP, units)
        result = sums_ref[start:end] + jnp.dot(held_ref[start:end, rest], rows, preferred_element_type=F32)
        result = result.T
        parts = [result[i * tokens : (i + 1) * tokens] for i in range(groups)]
        kept[:, start:end] = parts[0]
        far[:, start:end] = parts[-1].astype(BF16)
        early[:, start:end] = jnp.where(core == 0, parts[1], parts[-2]).astype(BF16)
        late[:, start:end] = jnp.where(core == 0, parts[-2], parts[1])
        for ref, part in zip(nears, parts[2:-2]):
            ref[:, start:end] = part.astype(BF16)


def add_kernel(late, came, out):
    out[...] = (late[...] + came[...].astype(F32)).astype(BF16)


def token_coefs(groups, new_ref, tables):
    own = positions()[0]
    lanes = tables[0].shape[1]
    ordered = []
    for j in range(groups):
        table = tables[0]
        for d in range(1, groups):
            table = jnp.where((own ^ j) == d, tables[d], table)
        ordered.append(table)
    length = new_ref.shape[2]
    place = lax.broadcasted_iota(jnp.int32, (1, lanes), 1)
    diagonal = lax.broadcasted_iota(jnp.int32, (length, lanes), 0) == lax.broadcasted_iota(jnp.int32, (length, lanes), 1)
    new = new_ref[0]
    new = jnp.concatenate([new, jnp.zeros((groups, lanes - length), F32)], axis=1)
    together = COMP // groups
    parts = []
    loss = jnp.zeros((1, lanes), F32)
    for j in range(groups):
        prompt = ordered[j // together * together : (j // together + 1) * together]
        mean = sum(table[3:4] for table in prompt) / COMP
        square = sum(table[4:5] for table in prompt) / COMP
        spread = jnp.sqrt(jnp.maximum(square - mean * mean, SPREAD_FLOOR))
        old, reward, count = ordered[j][0:1], ordered[j][1:2], ordered[j][2:3]
        advantage = (reward - mean) / spread
        ratio = jnp.exp(new[j : j + 1] - old)
        live = (place.astype(F32) < count) & (place < length)
        coef = jnp.where(live, -(advantage * ratio) / (count * COMP), 0.0)
        loss = loss + coef
        column = jnp.sum(jnp.where(diagonal, coef, 0.0), axis=1, keepdims=True)
        parts.append(column)
    return jnp.concatenate(parts, axis=0), jnp.sum(loss, axis=1, keepdims=True)


def adapter_kernel(groups, share, ride_rows, *refs):
    lows, (back_ref, new_ref, upstream_ref) = refs[:groups][::-1], refs[groups : groups + 3]
    messages, (own_term, own_back, low_ref, loss_ref, term) = refs[groups + 3 : 2 * groups + 2], refs[2 * groups + 2 :]
    own = positions()[0]
    rank = term.shape[0]
    tokens = back_ref.shape[0]
    coef, loss_ref[...] = token_coefs(groups, new_ref, [ref[tokens:] for ref in lows])
    low = lows[0][:tokens]
    for ref in lows[1:]:
        low = low + ref[:tokens]
    low = low.astype(BF16)
    low_ref[...] = low
    gradient = (coef * upstream_ref[...].astype(F32)).astype(BF16)
    term[...] = ADAPTER_SCALING * lax.dot_general(low, gradient, TN, preferred_element_type=F32)
    back = coef * back_ref[...]
    own_back[...] = back.astype(BF16)
    stack = back.shape[0] // ride_rows
    ride = jnp.concatenate([back[i * ride_rows : (i + 1) * ride_rows] for i in range(stack)], axis=1).astype(BF16)
    lanes = stack * rank
    for d in range(groups):
        if share % 8 == 0:
            piece = term[pl.ds(pl.multiple_of((own ^ d) * share, share), share), :]
        else:
            piece = term[:share]
            for j in range(1, groups):
                piece = jnp.where((own ^ d) == j, term[j * share : (j + 1) * share], piece)
        if d == 0:
            own_term[...] = piece
            continue
        if share < ride_rows:
            piece = jnp.concatenate([piece, jnp.zeros((ride_rows - share, piece.shape[1]), F32)], axis=0)
        messages[d - 1][:, :lanes] = ride
        messages[d - 1][:, lanes:] = piece.astype(BF16)


def output_kernel(total_ref, low_ref, up_ref, *rest):
    total = total_ref[...] + ADAPTER_SCALING * jnp.dot(low_ref[...], up_ref[...], preferred_element_type=F32)
    for ref in rest[:-2]:
        total = total + ref[...].astype(F32)
    rest[-2][...] = total.astype(BF16)
    rest[-1][...] = jnp.zeros_like(rest[-1])


def gradient_kernel(groups, rank, share, ride_rows, written, own_term, own_back, own_hidden, *rest):
    arrived, messages, others = (rest[i * (groups - 1) : (i + 1) * (groups - 1)][::-1] for i in range(3))
    up_hbm, down_hbm, up_ref, down_ref, sems = rest[3 * (groups - 1) :]
    core = positions()[2]
    tokens, depth = own_hidden.shape
    half = depth // 2
    stack = tokens // ride_rows
    lanes = stack * rank
    backs = [own_back[...].astype(F32)]
    for come in arrived:
        ride = come[:, :lanes].astype(F32)
        backs += [ride[:, i * rank : (i + 1) * rank] for i in range(stack)]
    back = jnp.concatenate(backs, axis=0).astype(BF16)
    copies = []
    for i in range(2):
        span = slice(i * half, (i + 1) * half)
        rows = [own_hidden[:, span]]
        rows += [jnp.where(core == i, a[...], b[...]) for a, b in zip(messages, others)]
        rows = jnp.concatenate(rows, axis=0)
        down_ref[:, span] = ADAPTER_SCALING * lax.dot_general(back, rows, TN, preferred_element_type=F32)
        copies += start_all([(down_ref.at[:, span], down_hbm.at[:, span])], sems, i)
    total = own_term[...]
    for come in arrived:
        total = total + come[:, lanes:].astype(F32)[:share]
    up_ref[...] = total
    copies += start_all([(up_ref, up_hbm)], sems, 2)
    for copy in copies:
        copy.wait()


def on_device(
    hidden_input_slots,
    base_weight,
    adapter_a,
    adapter_up_matrix,
    upstream,
    logp_new,
    logp_old,
    rewards,
    comp_lengths,
    assignment,
):
    groups = lax.axis_size("group")
    tokens = hidden_input_slots.shape[0]
    depth, units = base_weight.shape
    half = depth // 2
    rank = adapter_a.shape[1]
    others = range(1, groups)
    at, weight = adapter_a.T, base_weight.T

    *messages, table, own_hidden, new, at, upstream, up, back = call(
        functools.partial(pack_kernel, groups, depth),
        "pack",
        1.8,
        [pltpu.VMEM((tokens, half), BF16)] * (groups - 1)
        + [
            pltpu.VMEM((groups * BLOCK, LANES), F32),
            pltpu.VMEM((tokens, depth), BF16),
            pltpu.VMEM(logp_new.shape, F32),
            pltpu.VMEM((rank, depth), BF16),
            pltpu.VMEM((tokens, units), BF16),
            pltpu.VMEM((rank, units), BF16),
            pltpu.VMEM((tokens, rank), F32),
        ],
        [HBM] * 9,
        scratch=[
            pltpu.VMEM(logp_old.shape, F32),
            pltpu.SMEM(rewards.shape, F32),
            pltpu.SMEM(comp_lengths.shape, jnp.int32),
            pltpu.SMEM(assignment.shape, jnp.int32),
            pltpu.SemaphoreType.DMA((groups + 2,)),
            pltpu.SemaphoreType.DMA((6,)),
        ],
    )(
        *map(
            in_hbm,
            (
                hidden_input_slots,
                logp_old,
                rewards,
                comp_lengths,
                assignment,
                logp_new,
                at,
                upstream,
                adapter_up_matrix,
            ),
        )
    )
    got = {d: swap(messages[d - 1], "group", d) for d in reversed(others)}
    held = pltpu.with_memory_space_constraint(weight, pltpu.VMEM)
    far, near = groups - 1, list(range(1, groups - 1))
    held_sums, held_lows = call(
        first_kernel,
        "first",
        1.5,
        [pltpu.VMEM((units, groups * tokens), F32), pltpu.VMEM((groups * tokens, rank), F32)],
        [VMEM] * (2 + groups),
    )(held, at, own_hidden, *[got[d] for d in reversed(others)])
    back = sum_over_fsdp(back, held_lows)
    theirs = {d: swap(got[d], "fsdp", 1) for d in reversed(others)}
    far_term, early, late, kept, *terms = call(
        functools.partial(second_kernel, groups),
        "second",
        1.5,
        [
            pltpu.VMEM((tokens, units), BF16),
            pltpu.VMEM((tokens, units), BF16),
            pltpu.VMEM((tokens, units), F32),
            pltpu.VMEM((tokens, units), F32),
        ]
        + [pltpu.VMEM((tokens, units), BF16)] * (groups - 4)
        + [pltpu.VMEM((tokens + BLOCK, rank), F32)] * groups,
        [VMEM] * (5 + groups),
    )(held, at, own_hidden, table, held_sums, held_lows, *[theirs[d] for d in reversed(others)])
    own_low, *lows = terms[groups - 4 :]
    came = [swap(term, "group", d) for d, term in enumerate(terms[: groups - 4], 2)]
    ways = (1, far ^ 1)
    far_term = swap_pair(far_term, ways)
    came.append(swap_pair(early, ways))
    lows = [swap(lows[d - 1], "group", d) for d in reversed(others)][::-1]
    (late,) = call(add_kernel, "add", 0.5, [pltpu.VMEM((tokens, units), BF16)], [VMEM] * 2)(late, far_term)
    came.append(swap_pair(late, ways[::-1]))

    share = rank // groups
    ride_rows = max(share, 16)
    lanes = tokens // ride_rows * rank
    *pieces, own_term, own_back, low, loss = call(
        functools.partial(adapter_kernel, groups, share, ride_rows),
        "adapter",
        4.0,
        [pltpu.VMEM((ride_rows, lanes + units), BF16)] * (groups - 1)
        + [
            pltpu.VMEM((share, units), F32),
            pltpu.VMEM((tokens, rank), BF16),
            pltpu.VMEM((tokens, rank), BF16),
            jax.ShapeDtypeStruct((1, 1), F32),
        ],
        [VMEM] * (groups + 3),
        scratch=[pltpu.VMEM((rank, units), F32)],
    )(*lows[::-1], own_low, back, new, upstream)
    arrived = {d: swap(pieces[d - 1], "group", d) for d in reversed(others)}
    projection_output, written = call(
        output_kernel,
        "output",
        1.0,
        [jax.ShapeDtypeStruct((tokens, units), BF16), pltpu.VMEM((8, LANES), F32)],
        [VMEM] * (3 + len(came)),
    )(kept, low, up, *came)
    gradient_up, gradient_down = call(
        functools.partial(gradient_kernel, groups, rank, share, ride_rows),
        "gradient",
        1.2,
        [jax.ShapeDtypeStruct((share, units), F32), jax.ShapeDtypeStruct((rank, depth), F32)],
        [ANY] + [VMEM] * (3 * groups),
        scratch=[
            pltpu.VMEM((share, units), F32),
            pltpu.VMEM((rank, depth), F32),
            pltpu.SemaphoreType.DMA((3,)),
        ],
        out_specs=[HBM] * 2,
    )(
        written,
        own_term,
        own_back,
        own_hidden,
        *[arrived[d] for d in reversed(others)],
        *[got[d] for d in reversed(others)],
        *[theirs[d] for d in reversed(others)],
    )
    return (projection_output, gradient_down.T, gradient_up, loss[0])


def solution(mesh):
    return jax.shard_map(
        on_device,
        mesh=mesh,
        in_specs=(
            P("group", None),
            P("group", "fsdp"),
            P("group", None),
            P(None, "fsdp"),
            P("group", "fsdp"),
            P("group", None, None),
            P("group", None, None),
            P("group", None),
            P("group", None),
            P("group", None),
        ),
        out_specs=(P("group", "fsdp"), P("group", None), P("group", "fsdp"), P("group")),
        check_vma=False,
    )
```

```python
import functools

import jax
import jax.numpy as jnp
from jax import lax
from jax.experimental import pallas as pl
from jax.experimental.pallas import tpu as pltpu
from jax.sharding import PartitionSpec as P

COMP = 16


ADAPTER_SCALING = 0.25
SPREAD_FLOOR = 0.16
F32 = jnp.float32
BF16 = jnp.bfloat16
LANES = 128
BLOCK = 8
PEAK_FLOPS, PEAK_BYTES = 1.15e9, 3.6e6
STEP = 512
NT = (((1,), (1,)), ((), ()))
TN = (((0,), (0,)), ((), ()))
VMEM = pl.BlockSpec(memory_space=pltpu.VMEM)
SMEM = pl.BlockSpec(memory_space=pltpu.SMEM)
HBM = pl.BlockSpec(memory_space=pltpu.HBM)
ANY = pl.BlockSpec(memory_space=pl.ANY)


def swap(array, axis, distance):
    size = lax.axis_size(axis)
    return lax.ppermute(array, axis, [(i, i ^ distance) for i in range(size)])


def swap_cores(array, axis, partner):
    size = lax.axis_size(axis)
    return lax.ppermute(array, axis, [(i, i ^ partner[i % 2]) for i in range(size)])


def swap_pair(array, partner):
    groups, size = lax.axis_size("group"), lax.axis_size("fsdp")
    return lax.ppermute(
        array,
        ("group", "fsdp"),
        [(g * size + f, (g ^ partner[f % 2]) * size + f) for g in range(groups) for f in range(size)],
    )


def sum_over_fsdp(partial, earlier, later):
    size = lax.axis_size("fsdp")
    if size & (size - 1):
        return lax.psum(partial, "fsdp")
    chip = partial + swap(partial, "fsdp", 1)
    if size == 8:
        one = swap_cores(chip, "fsdp", (2, 4))
        chip = after(chip, earlier) + swap(chip, "fsdp", 6)
        return chip + (one + swap(after(one, earlier), "fsdp", 1))
    parts = [chip] + [swap(chip, "fsdp", d) for d in range(2, size, 2)]
    while len(parts) > 1:
        parts = [parts[i] + parts[i + 1] for i in range(0, len(parts), 2)]
    return parts[0]


def after(array, earlier):
    return lax.optimization_barrier((array, earlier))[0]


def call(body, name, cost, outs, ins, scratch=(), out_specs=None):
    return pl.pallas_call(
        body,
        out_shape=outs,
        in_specs=ins,
        out_specs=out_specs or [VMEM] * len(outs),
        scratch_shapes=scratch,
        compiler_params=pltpu.CompilerParams(vmem_limit_bytes=8 << 20),
        cost_estimate=pl.CostEstimate(
            flops=int(cost * PEAK_FLOPS), bytes_accessed=int(cost * PEAK_BYTES), transcendentals=0
        ),
        name=name,
    )


def in_hbm(array):
    return pltpu.with_memory_space_constraint(array, pltpu.HBM)


def positions():
    own, member = lax.axis_index("group"), lax.axis_index("fsdp")
    return own, member, lax.rem(member, 2)


def start_all(pairs, sems, first=0):
    copies = [pltpu.make_async_copy(a, b, sems.at[first + i]) for i, (a, b) in enumerate(pairs)]
    for copy in copies:
        copy.start()
    return copies


def pack_kernel(groups, depth, hidden_ref, old_hbm, reward_hbm, length_hbm, dest_hbm, new_hbm, at_hbm, upstream_hbm, up_hbm, *rest):
    messages, tail_ref, own_hidden = rest[: groups - 1], rest[groups - 1], rest[groups]
    at_ref, upstream_ref, up_ref, back_ref = rest[groups + 1 : groups + 5]
    old_ref, new_ref, reward_ref, length_ref, dest_ref, sems, small_sems = rest[groups + 5 :]
    own, _, core = positions()
    half = depth // 2
    small = [(old_hbm, old_ref), (reward_hbm, reward_ref), (length_hbm, length_ref), (dest_hbm, dest_ref)]
    small += [(new_hbm, new_ref), (upstream_hbm, upstream_ref), (up_hbm, up_ref)]
    small = start_all(small, small_sems)
    pairs = []
    for d in reversed(range(1, groups)):
        start = pl.multiple_of((own ^ d) * depth + core * half, LANES)
        pairs.append((hidden_ref.at[:, pl.ds(start, half)], messages[d - 1]))
    pairs.append((hidden_ref.at[:, pl.ds(pl.multiple_of(own * depth, LANES), depth)], own_hidden))
    copies = start_all(pairs + [(at_hbm, at_ref)], sems)
    for copy in small:
        copy.wait()
    total, squares = jnp.float32(0), jnp.float32(0)
    for k in range(groups):
        total += reward_ref[0, k]
        squares += reward_ref[0, k] * reward_ref[0, k]
    length = old_ref.shape[2]
    lanes = -(-groups * length // LANES) * LANES
    place = lax.broadcasted_iota(jnp.int32, (1, lanes), 1)
    old, new = (jnp.concatenate([ref[0]] * (lanes // length), axis=1) for ref in (old_ref, new_ref))
    line, reward, count = (jnp.zeros((1, lanes), F32) for _ in range(3))
    for k in range(groups):
        start = dest_ref[0, k] * length
        chosen = (place >= start) & (place < start + length)
        line = jnp.where(chosen, old[k : k + 1], line)
        reward = jnp.where(chosen, reward_ref[0, k], reward)
        count = jnp.where(chosen, length_ref[0, k].astype(F32), count)
    lines = [line, reward, count] + [jnp.full((1, lanes), x, F32) for x in (total, squares)]
    lines.append(jnp.zeros((BLOCK - len(lines), lanes), F32))
    chosen = (place >= own * length) & (place < (own + 1) * length)
    lines.append(jnp.where(chosen, new, 0.0))
    if groups % BLOCK:
        lines.append(jnp.zeros((BLOCK - groups % BLOCK, lanes), F32))
    value = jnp.concatenate(lines, axis=0)
    rows = value.shape[0]
    for i in range(lanes // LANES):
        tail_ref[i * rows : (i + 1) * rows] = value[:, i * LANES : (i + 1) * LANES]
    back_ref[...] = lax.dot_general(upstream_ref[...], up_ref[...], NT, preferred_element_type=F32)
    for copy in copies:
        copy.wait()


def whole_rows(half, core, message, other):
    a, b = message[:, :half], other[:, :half]
    first = core == 0
    return jnp.concatenate([jnp.where(first, a, b), jnp.where(first, b, a)], axis=1)


def first_kernel(held_ref, at_ref, own_hidden, *refs):
    *messages, sums_ref, low_ref = refs
    messages = messages[::-1]
    units, depth = held_ref.shape
    half = depth // 2
    mine = pl.ds(pl.multiple_of(positions()[2] * half, LANES), half)
    rows = jnp.concatenate([own_hidden[:, mine]] + [ref[...] for ref in messages], axis=0)
    low_ref[...] = lax.dot_general(rows, at_ref[:, mine], NT, preferred_element_type=F32)
    rows = rows.T
    for start in range(0, units, STEP):
        end = min(start + STEP, units)
        sums_ref[start:end] = jnp.dot(held_ref[start:end, mine], rows, preferred_element_type=F32)


def second_kernel(groups, held_ref, at_ref, own_hidden, sums_ref, low_ref, *refs):
    count = groups - 1
    others, refs = refs[:count][::-1], refs[count:]
    far, early, late, kept, nears, lows = *refs[:4], refs[4 : groups], refs[groups:]
    units, depth = held_ref.shape
    tokens, rank = own_hidden.shape[0], low_ref.shape[1]
    half = depth // 2
    core = positions()[2]
    rest = pl.ds(pl.multiple_of((1 - core) * half, LANES), half)
    rows = jnp.concatenate([own_hidden[:, rest]] + [ref[...] for ref in others], axis=0)
    low = low_ref[...] + lax.dot_general(rows, at_ref[:, rest], NT, preferred_element_type=F32)
    for i, ref in enumerate(lows):
        ref[...] = low[i * tokens : (i + 1) * tokens]
    rows = rows.T
    for start in range(0, units, STEP):
        end = min(start + STEP, units)
        result = sums_ref[start:end] + jnp.dot(held_ref[start:end, rest], rows, preferred_element_type=F32)
        result = result.T
        parts = [result[i * tokens : (i + 1) * tokens] for i in range(groups)]
        kept[:, start:end] = parts[0]
        far[:, start:end] = parts[-1].astype(BF16)
        early[:, start:end] = jnp.where(core == 0, parts[1], parts[-2]).astype(BF16)
        late[:, start:end] = jnp.where(core == 0, parts[-2], parts[1])
        for ref, part in zip(nears, parts[2:-2]):
            ref[:, start:end] = part.astype(BF16)


def add_kernel(late, came, out):
    out[...] = (late[...] + came[...].astype(F32)).astype(BF16)


def letter_kernel(back_ref, tail_ref, *refs):
    count = len(refs) // 2
    tokens, rank = back_ref.shape
    for low, letter in zip(refs[:count], refs[count:]):
        letter[:tokens, :rank] = low[...]
        letter[:tokens, rank:] = back_ref[...]
        letter[tokens:] = tail_ref[...]


def token_coefs(groups, length, tails):
    own = positions()[0]
    chunks = -(-groups * length // LANES)
    rows = tails[0].shape[0] // chunks
    tails = [jnp.concatenate([tail[i * rows : (i + 1) * rows] for i in range(chunks)], axis=1) for tail in tails]
    new = sum(tail[BLOCK : BLOCK + groups] for tail in tails)
    ordered = []
    for j in range(groups):
        table = tails[0][:BLOCK]
        for d in range(1, groups):
            table = jnp.where((own ^ j) == d, tails[d][:BLOCK], table)
        ordered.append(table)
    lanes = new.shape[1]
    place = lax.broadcasted_iota(jnp.int32, (1, lanes), 1)
    together = COMP // groups
    means, squares = [], []
    for j in range(0, groups, together):
        prompt = ordered[j : j + together]
        means += [sum(table[3:4] for table in prompt) / COMP] * together
        squares += [sum(table[4:5] for table in prompt) / COMP] * together
    mean, square = jnp.concatenate(means, axis=0), jnp.concatenate(squares, axis=0)
    old, reward, count = (jnp.concatenate([table[i : i + 1] for table in ordered], axis=0) for i in range(3))
    spread = jnp.sqrt(jnp.maximum(square - mean * mean, SPREAD_FLOOR))
    advantage = (reward - mean) / spread
    ratio = jnp.exp(new - old)
    position = jnp.bitwise_and(place, length - 1).astype(F32)
    live = (position < count) & (place < groups * length)
    coef = jnp.where(live, -(advantage * ratio) / (jnp.maximum(count, 1.0) * COMP), 0.0)
    coef = jnp.concatenate([jnp.broadcast_to(coef[j : j + 1], (length, lanes)) for j in range(groups)], axis=0)
    row = jnp.concatenate([lax.broadcasted_iota(jnp.int32, (length, lanes), 0)] * groups, axis=0)
    offset = lax.broadcasted_iota(jnp.int32, (groups * length, lanes), 1) - row
    return [
        jnp.sum(jnp.where(offset == (own ^ d) * length, coef, 0.0), axis=1, keepdims=True) for d in range(groups)
    ]


def adapter_kernel(groups, length, share, own_low, own_back, own_tail, upstream_ref, *refs):
    count = groups - 1
    letters, messages, (own_term, back_ref, low_ref, loss_ref, term) = refs[:count][::-1], refs[count : 2 * count], refs[2 * count :]
    own = positions()[0]
    tokens, rank = own_back.shape
    coefs = token_coefs(groups, length, [own_tail[...]] + [ref[tokens:] for ref in letters])
    loss_ref[...] = jnp.sum(coefs[0], axis=0, keepdims=True)
    low = own_low[...]
    for ref in letters:
        low = low + ref[:tokens, :rank]
    low = low.astype(BF16)
    low_ref[...] = low
    gradient = (coefs[0] * upstream_ref[...].astype(F32)).astype(BF16)
    term[...] = ADAPTER_SCALING * lax.dot_general(low, gradient, TN, preferred_element_type=F32)
    backs = [own_back[...]] + [ref[:tokens, rank:] for ref in letters]
    for d in range(groups):
        back_ref[d * tokens : (d + 1) * tokens] = (coefs[d] * backs[d]).astype(BF16)
        if share % BLOCK == 0:
            piece = term[pl.ds(pl.multiple_of((own ^ d) * share, share), share), :]
        else:
            piece = term[:share]
            for j in range(1, groups):
                piece = jnp.where((own ^ d) == j, term[j * share : (j + 1) * share], piece)
        if d == 0:
            own_term[...] = piece
            continue
        rows = messages[d - 1].shape[0]
        if share < rows:
            piece = jnp.concatenate([piece, jnp.zeros((rows - share, piece.shape[1]), F32)], axis=0)
        messages[d - 1][...] = piece.astype(BF16)


def output_kernel(total_ref, low_ref, up_ref, *rest):
    total = total_ref[...] + ADAPTER_SCALING * jnp.dot(low_ref[...], up_ref[...], preferred_element_type=F32)
    for ref in rest[:-2]:
        total = total + ref[...].astype(F32)
    rest[-2][...] = total.astype(BF16)
    rest[-1][...] = jnp.zeros_like(rest[-1])


def down_kernel(back_ref, own_hidden, *rest):
    count = len(rest) // 2 - 1
    messages, others = rest[:count][::-1], rest[count : 2 * count][::-1]
    down_hbm, down_ref, sems = rest[2 * count :]
    core = positions()[2]
    half = own_hidden.shape[1] // 2
    copies = []
    for i in range(2):
        span = slice(i * half, (i + 1) * half)
        rows = [own_hidden[:, span]]
        rows += [jnp.where(core == i, a[...], b[...]) for a, b in zip(messages, others)]
        rows = jnp.concatenate(rows, axis=0)
        down_ref[:, span] = ADAPTER_SCALING * lax.dot_general(back_ref[...], rows, TN, preferred_element_type=F32)
        copies += start_all([(down_ref.at[:, span], down_hbm.at[:, span])], sems, i)
    for copy in copies:
        copy.wait()


def gradient_kernel(written, own_term, *rest):
    total = own_term[...]
    for come in rest[:-1]:
        total = total + come[...].astype(F32)[: total.shape[0]]
    rest[-1][...] = total


def on_device(
    hidden_input_slots,
    base_weight,
    adapter_a,
    adapter_up_matrix,
    upstream,
    logp_new,
    logp_old,
    rewards,
    comp_lengths,
    assignment,
):
    groups = lax.axis_size("group")
    tokens = hidden_input_slots.shape[0]
    depth, units = base_weight.shape
    half = depth // 2
    rank = adapter_a.shape[1]
    others = range(1, groups)
    at, weight = adapter_a.T, base_weight.T

    length = logp_new.shape[2]
    chunks = -(-groups * length // LANES)
    tail_rows = chunks * (BLOCK + -(-groups // BLOCK) * BLOCK)
    *messages, tail, own_hidden, at, upstream, up, back = call(
        functools.partial(pack_kernel, groups, depth),
        "pack",
        1.8,
        [pltpu.VMEM((tokens, half), BF16)] * (groups - 1)
        + [
            pltpu.VMEM((tail_rows, LANES), F32),
            pltpu.VMEM((tokens, depth), BF16),
            pltpu.VMEM((rank, depth), BF16),
            pltpu.VMEM((tokens, units), BF16),
            pltpu.VMEM((rank, units), BF16),
            pltpu.VMEM((tokens, rank), F32),
        ],
        [HBM] * 9,
        scratch=[
            pltpu.VMEM(logp_old.shape, F32),
            pltpu.VMEM(logp_new.shape, F32),
            pltpu.SMEM(rewards.shape, F32),
            pltpu.SMEM(comp_lengths.shape, jnp.int32),
            pltpu.SMEM(assignment.shape, jnp.int32),
            pltpu.SemaphoreType.DMA((groups + 1,)),
            pltpu.SemaphoreType.DMA((7,)),
        ],
    )(
        *map(
            in_hbm,
            (
                hidden_input_slots,
                logp_old,
                rewards,
                comp_lengths,
                assignment,
                logp_new,
                at,
                upstream,
                adapter_up_matrix,
            ),
        )
    )
    got = {d: swap(messages[d - 1], "group", d) for d in reversed(others)}
    held = pltpu.with_memory_space_constraint(weight, pltpu.VMEM)
    far, near = groups - 1, list(range(1, groups - 1))
    held_sums, held_lows = call(
        first_kernel,
        "first",
        1.5,
        [pltpu.VMEM((units, groups * tokens), F32), pltpu.VMEM((groups * tokens, rank), F32)],
        [VMEM] * (2 + groups),
    )(held, at, own_hidden, *[got[d] for d in reversed(others)])
    theirs = {d: swap(got[d], "fsdp", 1) for d in reversed(others)}
    far_term, early, late, kept, *terms = call(
        functools.partial(second_kernel, groups),
        "second",
        1.5,
        [
            pltpu.VMEM((tokens, units), BF16),
            pltpu.VMEM((tokens, units), BF16),
            pltpu.VMEM((tokens, units), F32),
            pltpu.VMEM((tokens, units), F32),
        ]
        + [pltpu.VMEM((tokens, units), BF16)] * (groups - 4)
        + [pltpu.VMEM((tokens, rank), F32)] * groups,
        [VMEM] * (4 + groups),
    )(held, at, own_hidden, held_sums, held_lows, *[theirs[d] for d in reversed(others)])
    own_low, *lows = terms[groups - 4 :]
    back = sum_over_fsdp(back, held_lows, own_low)
    came = [swap(term, "group", d) for d, term in enumerate(terms[: groups - 4], 2)]
    ways = (1, far ^ 1)
    far_term = swap_pair(far_term, ways)
    letters = call(
        letter_kernel,
        "letter",
        0.3,
        [pltpu.VMEM((tokens + tail_rows, 2 * rank), F32)] * (groups - 1),
        [VMEM] * (1 + groups),
    )(back, tail, *lows)
    letters = [swap(letters[d - 1], "group", d) for d in reversed(others)]
    came.append(swap_pair(early, ways))
    (late,) = call(add_kernel, "add", 0.5, [pltpu.VMEM((tokens, units), BF16)], [VMEM] * 2)(late, far_term)
    came.append(swap_pair(late, ways[::-1]))

    share = rank // groups
    ride_rows = max(share, 16)
    *pieces, own_term, back_all, low, loss = call(
        functools.partial(adapter_kernel, groups, length, share),
        "adapter",
        1.0,
        [pltpu.VMEM((ride_rows, units), BF16)] * (groups - 1)
        + [
            pltpu.VMEM((share, units), F32),
            pltpu.VMEM((groups * tokens, rank), BF16),
            pltpu.VMEM((tokens, rank), BF16),
            jax.ShapeDtypeStruct((1, 1), F32),
        ],
        [VMEM] * (groups + 3),
        scratch=[pltpu.VMEM((rank, units), F32)],
    )(own_low, back, tail, upstream, *letters)
    arrived = {d: swap(pieces[d - 1], "group", d) for d in reversed(others)}
    (gradient_down,) = call(
        down_kernel,
        "down",
        1.0,
        [jax.ShapeDtypeStruct((rank, depth), F32)],
        [VMEM] * (2 * groups),
        scratch=[pltpu.VMEM((rank, depth), F32), pltpu.SemaphoreType.DMA((2,))],
        out_specs=[HBM],
    )(back_all, own_hidden, *[got[d] for d in reversed(others)], *[theirs[d] for d in reversed(others)])
    projection_output, written = call(
        output_kernel,
        "output",
        1.0,
        [jax.ShapeDtypeStruct((tokens, units), BF16), pltpu.VMEM((8, LANES), F32)],
        [VMEM] * (3 + len(came)),
    )(kept, low, up, *came)
    (gradient_up,) = call(
        gradient_kernel,
        "gradient",
        2.5,
        [jax.ShapeDtypeStruct((share, units), F32)],
        [ANY] + [VMEM] * groups,
    )(written, own_term, *[arrived[d] for d in reversed(others)])
    return (projection_output, gradient_down.T, gradient_up, loss[0])


def solution(mesh):
    return jax.shard_map(
        on_device,
        mesh=mesh,
        in_specs=(
            P("group", None),
            P("group", "fsdp"),
            P("group", None),
            P(None, "fsdp"),
            P("group", "fsdp"),
            P("group", None, None),
            P("group", None, None),
            P("group", None),
            P("group", None),
            P("group", None),
        ),
        out_specs=(P("group", "fsdp"), P("group", None), P("group", "fsdp"), P("group")),
        check_vma=False,
    )
```

```python
import functools

import jax
import jax.numpy as jnp
from jax import lax
from jax.experimental import pallas as pl
from jax.experimental.pallas import tpu as pltpu
from jax.sharding import PartitionSpec as P

COMP = 16


ADAPTER_SCALING = 0.25
SPREAD_FLOOR = 0.16
F32 = jnp.float32
BF16 = jnp.bfloat16
LANES = 128
BLOCK = 8
PEAK_FLOPS, PEAK_BYTES = 1.15e9, 3.6e6
STEP = 512
NT = (((1,), (1,)), ((), ()))
TN = (((0,), (0,)), ((), ()))
VMEM = pl.BlockSpec(memory_space=pltpu.VMEM)
SMEM = pl.BlockSpec(memory_space=pltpu.SMEM)
HBM = pl.BlockSpec(memory_space=pltpu.HBM)
ANY = pl.BlockSpec(memory_space=pl.ANY)


def swap(array, axis, distance):
    size = lax.axis_size(axis)
    return lax.ppermute(array, axis, [(i, i ^ distance) for i in range(size)])


def swap_cores(array, axis, partner):
    size = lax.axis_size(axis)
    return lax.ppermute(array, axis, [(i, i ^ partner[i % 2]) for i in range(size)])


def swap_pair(array, partner):
    groups, size = lax.axis_size("group"), lax.axis_size("fsdp")
    return lax.ppermute(
        array,
        ("group", "fsdp"),
        [(g * size + f, (g ^ partner[f % 2]) * size + f) for g in range(groups) for f in range(size)],
    )


def sum_over_fsdp(partial, earlier, later):
    size = lax.axis_size("fsdp")
    if size & (size - 1):
        return lax.psum(partial, "fsdp")
    chip = partial + swap(partial, "fsdp", 1)
    if size == 8:
        one = swap_cores(chip, "fsdp", (2, 4))
        chip = after(chip, earlier) + swap(chip, "fsdp", 6)
        return chip + (one + swap(after(one, earlier), "fsdp", 1))
    parts = [chip] + [swap(chip, "fsdp", d) for d in range(2, size, 2)]
    while len(parts) > 1:
        parts = [parts[i] + parts[i + 1] for i in range(0, len(parts), 2)]
    return parts[0]


def after(array, earlier):
    return lax.optimization_barrier((array, earlier))[0]


def call(body, name, cost, outs, ins, scratch=(), out_specs=None):
    return pl.pallas_call(
        body,
        out_shape=outs,
        in_specs=ins,
        out_specs=out_specs or [VMEM] * len(outs),
        scratch_shapes=scratch,
        compiler_params=pltpu.CompilerParams(vmem_limit_bytes=8 << 20),
        cost_estimate=pl.CostEstimate(
            flops=int(cost * PEAK_FLOPS), bytes_accessed=int(cost * PEAK_BYTES), transcendentals=0
        ),
        name=name,
    )


def in_hbm(array):
    return pltpu.with_memory_space_constraint(array, pltpu.HBM)


def positions():
    own, member = lax.axis_index("group"), lax.axis_index("fsdp")
    return own, member, lax.rem(member, 2)


def start_all(pairs, sems, first=0):
    copies = [pltpu.make_async_copy(a, b, sems.at[first + i]) for i, (a, b) in enumerate(pairs)]
    for copy in copies:
        copy.start()
    return copies


def pack_kernel(groups, depth, hidden_ref, old_hbm, reward_hbm, length_hbm, dest_hbm, new_hbm, at_hbm, upstream_hbm, up_hbm, *rest):
    messages, tail_ref, own_hidden = rest[: groups - 1], rest[groups - 1], rest[groups]
    at_ref, upstream_ref, up_ref, back_ref = rest[groups + 1 : groups + 5]
    old_ref, new_ref, reward_ref, length_ref, dest_ref, sems, small_sems = rest[groups + 5 :]
    own, _, core = positions()
    half = depth // 2
    small = [(old_hbm, old_ref), (reward_hbm, reward_ref), (length_hbm, length_ref), (dest_hbm, dest_ref)]
    small += [(new_hbm, new_ref), (upstream_hbm, upstream_ref), (up_hbm, up_ref)]
    small = start_all(small, small_sems)
    pairs = []
    for d in reversed(range(1, groups)):
        start = pl.multiple_of((own ^ d) * depth + core * half, LANES)
        pairs.append((hidden_ref.at[:, pl.ds(start, half)], messages[d - 1]))
    pairs.append((hidden_ref.at[:, pl.ds(pl.multiple_of(own * depth, LANES), depth)], own_hidden))
    copies = start_all(pairs + [(at_hbm, at_ref)], sems)
    for copy in small:
        copy.wait()
    total, squares = jnp.float32(0), jnp.float32(0)
    for k in range(groups):
        total += reward_ref[0, k]
        squares += reward_ref[0, k] * reward_ref[0, k]
    length = old_ref.shape[2]
    lanes = -(-groups * length // LANES) * LANES
    place = lax.broadcasted_iota(jnp.int32, (1, lanes), 1)
    old, new = (jnp.concatenate([ref[0]] * (lanes // length), axis=1) for ref in (old_ref, new_ref))
    line, reward, count = (jnp.zeros((1, lanes), F32) for _ in range(3))
    for k in range(groups):
        start = dest_ref[0, k] * length
        chosen = (place >= start) & (place < start + length)
        line = jnp.where(chosen, old[k : k + 1], line)
        reward = jnp.where(chosen, reward_ref[0, k], reward)
        count = jnp.where(chosen, length_ref[0, k].astype(F32), count)
    lines = [line, reward, count] + [jnp.full((1, lanes), x, F32) for x in (total, squares)]
    lines.append(jnp.zeros((BLOCK - len(lines), lanes), F32))
    chosen = (place >= own * length) & (place < (own + 1) * length)
    lines.append(jnp.where(chosen, new, 0.0))
    if groups % BLOCK:
        lines.append(jnp.zeros((BLOCK - groups % BLOCK, lanes), F32))
    value = jnp.concatenate(lines, axis=0)
    rows = value.shape[0]
    for i in range(lanes // LANES):
        tail_ref[i * rows : (i + 1) * rows] = value[:, i * LANES : (i + 1) * LANES]
    back_ref[...] = lax.dot_general(upstream_ref[...], up_ref[...], NT, preferred_element_type=F32)
    for copy in copies:
        copy.wait()


def whole_rows(half, core, message, other):
    a, b = message[:, :half], other[:, :half]
    first = core == 0
    return jnp.concatenate([jnp.where(first, a, b), jnp.where(first, b, a)], axis=1)


def first_kernel(held_ref, at_ref, own_hidden, *refs):
    *messages, sums_ref, low_ref = refs
    messages = messages[::-1]
    units, depth = held_ref.shape
    half = depth // 2
    mine = pl.ds(pl.multiple_of(positions()[2] * half, LANES), half)
    rows = jnp.concatenate([own_hidden[:, mine]] + [ref[...] for ref in messages], axis=0)
    low_ref[...] = lax.dot_general(rows, at_ref[:, mine], NT, preferred_element_type=F32)
    rows = rows.T
    for start in range(0, units, STEP):
        end = min(start + STEP, units)
        sums_ref[start:end] = jnp.dot(held_ref[start:end, mine], rows, preferred_element_type=F32)


def second_kernel(groups, held_ref, at_ref, own_hidden, sums_ref, low_ref, *refs):
    count = groups - 1
    others, refs = refs[:count][::-1], refs[count:]
    far, early, late, kept, nears, lows = *refs[:4], refs[4 : groups], refs[groups:]
    units, depth = held_ref.shape
    tokens, rank = own_hidden.shape[0], low_ref.shape[1]
    half = depth // 2
    core = positions()[2]
    rest = pl.ds(pl.multiple_of((1 - core) * half, LANES), half)
    rows = jnp.concatenate([own_hidden[:, rest]] + [ref[...] for ref in others], axis=0)
    low = low_ref[...] + lax.dot_general(rows, at_ref[:, rest], NT, preferred_element_type=F32)
    for i, ref in enumerate(lows):
        ref[...] = low[i * tokens : (i + 1) * tokens]
    rows = rows.T
    for start in range(0, units, STEP):
        end = min(start + STEP, units)
        result = sums_ref[start:end] + jnp.dot(held_ref[start:end, rest], rows, preferred_element_type=F32)
        result = result.T
        parts = [result[i * tokens : (i + 1) * tokens] for i in range(groups)]
        kept[:, start:end] = parts[0]
        far[:, start:end] = parts[-1].astype(BF16)
        early[:, start:end] = jnp.where(core == 0, parts[1], parts[-2]).astype(BF16)
        late[:, start:end] = jnp.where(core == 0, parts[-2], parts[1])
        for ref, part in zip(nears, parts[2:-2]):
            ref[:, start:end] = part.astype(BF16)


def add_kernel(late, came, out):
    out[...] = (late[...] + came[...].astype(F32)).astype(BF16)


def letter_kernel(back_ref, tail_ref, *refs):
    count = len(refs) // 2
    tokens, rank = back_ref.shape
    for low, letter in zip(refs[:count], refs[count:]):
        letter[:tokens, :rank] = low[...]
        letter[:tokens, rank:] = back_ref[...]
        letter[tokens:] = tail_ref[...]


def token_coefs(groups, length, tails):
    own = positions()[0]
    chunks = -(-groups * length // LANES)
    rows = tails[0].shape[0] // chunks
    tails = [jnp.concatenate([tail[i * rows : (i + 1) * rows] for i in range(chunks)], axis=1) for tail in tails]
    new = sum(tail[BLOCK : BLOCK + groups] for tail in tails)
    ordered = []
    for j in range(groups):
        table = tails[0][:BLOCK]
        for d in range(1, groups):
            table = jnp.where((own ^ j) == d, tails[d][:BLOCK], table)
        ordered.append(table)
    lanes = new.shape[1]
    place = lax.broadcasted_iota(jnp.int32, (1, lanes), 1)
    together = COMP // groups
    means, squares = [], []
    for j in range(0, groups, together):
        prompt = ordered[j : j + together]
        means += [sum(table[3:4] for table in prompt) / COMP] * together
        squares += [sum(table[4:5] for table in prompt) / COMP] * together
    mean, square = jnp.concatenate(means, axis=0), jnp.concatenate(squares, axis=0)
    old, reward, count = (jnp.concatenate([table[i : i + 1] for table in ordered], axis=0) for i in range(3))
    spread = jnp.sqrt(jnp.maximum(square - mean * mean, SPREAD_FLOOR))
    advantage = (reward - mean) / spread
    ratio = jnp.exp(new - old)
    position = jnp.bitwise_and(place, length - 1).astype(F32)
    live = (position < count) & (place < groups * length)
    coef = jnp.where(live, -(advantage * ratio) / (jnp.maximum(count, 1.0) * COMP), 0.0)
    return jnp.concatenate([jnp.broadcast_to(coef[j : j + 1], (length, lanes)) for j in range(groups)], axis=0)


def coef_column(groups, length, target, coefs):
    row = jnp.concatenate([lax.broadcasted_iota(jnp.int32, (length, coefs.shape[1]), 0)] * groups, axis=0)
    offset = lax.broadcasted_iota(jnp.int32, coefs.shape, 1) - row
    return jnp.sum(jnp.where(offset == target * length, coefs, 0.0), axis=1, keepdims=True)


def adapter_kernel(groups, length, share, own_low, own_tail, upstream_ref, *refs):
    count = groups - 1
    letters, messages, (own_term, coef_ref, low_ref, term) = refs[:count][::-1], refs[count : 2 * count], refs[2 * count :]
    own = positions()[0]
    tokens, rank = own_low.shape
    coefs = token_coefs(groups, length, [own_tail[...]] + [ref[tokens:] for ref in letters])
    coef_ref[...] = coefs
    coef = coef_column(groups, length, own, coefs)
    low = own_low[...]
    for ref in letters:
        low = low + ref[:tokens, :rank]
    low = low.astype(BF16)
    low_ref[...] = low
    gradient = (coef * upstream_ref[...].astype(F32)).astype(BF16)
    term[...] = ADAPTER_SCALING * lax.dot_general(low, gradient, TN, preferred_element_type=F32)
    for d in range(groups):
        if share % BLOCK == 0:
            piece = term[pl.ds(pl.multiple_of((own ^ d) * share, share), share), :]
        else:
            piece = term[:share]
            for j in range(1, groups):
                piece = jnp.where((own ^ d) == j, term[j * share : (j + 1) * share], piece)
        if d == 0:
            own_term[...] = piece
            continue
        rows = messages[d - 1].shape[0]
        if share < rows:
            piece = jnp.concatenate([piece, jnp.zeros((rows - share, piece.shape[1]), F32)], axis=0)
        messages[d - 1][...] = piece.astype(BF16)


def output_kernel(total_ref, low_ref, up_ref, *rest):
    total = total_ref[...] + ADAPTER_SCALING * jnp.dot(low_ref[...], up_ref[...], preferred_element_type=F32)
    for ref in rest[:-2]:
        total = total + ref[...].astype(F32)
    rest[-2][...] = total.astype(BF16)
    rest[-1][...] = jnp.zeros_like(rest[-1])


def down_kernel(groups, length, coef_ref, own_back, own_hidden, *rest):
    count = groups - 1
    letters, messages, others = (rest[i * count : (i + 1) * count][::-1] for i in range(3))
    down_hbm, loss_ref, down_ref, sems = rest[3 * count :]
    own = positions()[0]
    tokens, rank = own_back.shape
    coefs = coef_ref[...]
    backs = [own_back[...]] + [ref[:tokens, rank:] for ref in letters]
    columns = [coef_column(groups, length, own ^ d, coefs) for d in range(groups)]
    loss_ref[...] = jnp.sum(columns[0], axis=0, keepdims=True)
    back = jnp.concatenate([column * part for column, part in zip(columns, backs)], axis=0).astype(BF16)
    core = positions()[2]
    half = own_hidden.shape[1] // 2
    copies = []
    for i in range(2):
        span = slice(i * half, (i + 1) * half)
        rows = [own_hidden[:, span]]
        rows += [jnp.where(core == i, a[...], b[...]) for a, b in zip(messages, others)]
        rows = jnp.concatenate(rows, axis=0)
        down_ref[:, span] = ADAPTER_SCALING * lax.dot_general(back, rows, TN, preferred_element_type=F32)
        copies += start_all([(down_ref.at[:, span], down_hbm.at[:, span])], sems, i)
    for copy in copies:
        copy.wait()


def gradient_kernel(written, own_term, *rest):
    total = own_term[...]
    for come in rest[:-1]:
        total = total + come[...].astype(F32)[: total.shape[0]]
    rest[-1][...] = total


def on_device(
    hidden_input_slots,
    base_weight,
    adapter_a,
    adapter_up_matrix,
    upstream,
    logp_new,
    logp_old,
    rewards,
    comp_lengths,
    assignment,
):
    groups = lax.axis_size("group")
    tokens = hidden_input_slots.shape[0]
    depth, units = base_weight.shape
    half = depth // 2
    rank = adapter_a.shape[1]
    others = range(1, groups)
    at, weight = adapter_a.T, base_weight.T

    length = logp_new.shape[2]
    chunks = -(-groups * length // LANES)
    tail_rows = chunks * (BLOCK + -(-groups // BLOCK) * BLOCK)
    *messages, tail, own_hidden, at, upstream, up, back = call(
        functools.partial(pack_kernel, groups, depth),
        "pack",
        1.8,
        [pltpu.VMEM((tokens, half), BF16)] * (groups - 1)
        + [
            pltpu.VMEM((tail_rows, LANES), F32),
            pltpu.VMEM((tokens, depth), BF16),
            pltpu.VMEM((rank, depth), BF16),
            pltpu.VMEM((tokens, units), BF16),
            pltpu.VMEM((rank, units), BF16),
            pltpu.VMEM((tokens, rank), F32),
        ],
        [HBM] * 9,
        scratch=[
            pltpu.VMEM(logp_old.shape, F32),
            pltpu.VMEM(logp_new.shape, F32),
            pltpu.SMEM(rewards.shape, F32),
            pltpu.SMEM(comp_lengths.shape, jnp.int32),
            pltpu.SMEM(assignment.shape, jnp.int32),
            pltpu.SemaphoreType.DMA((groups + 1,)),
            pltpu.SemaphoreType.DMA((7,)),
        ],
    )(
        *map(
            in_hbm,
            (
                hidden_input_slots,
                logp_old,
                rewards,
                comp_lengths,
                assignment,
                logp_new,
                at,
                upstream,
                adapter_up_matrix,
            ),
        )
    )
    got = {d: swap(messages[d - 1], "group", d) for d in reversed(others)}
    held = pltpu.with_memory_space_constraint(weight, pltpu.VMEM)
    far, near = groups - 1, list(range(1, groups - 1))
    held_sums, held_lows = call(
        first_kernel,
        "first",
        1.5,
        [pltpu.VMEM((units, groups * tokens), F32), pltpu.VMEM((groups * tokens, rank), F32)],
        [VMEM] * (2 + groups),
    )(held, at, own_hidden, *[got[d] for d in reversed(others)])
    theirs = {d: swap(got[d], "fsdp", 1) for d in reversed(others)}
    far_term, early, late, kept, *terms = call(
        functools.partial(second_kernel, groups),
        "second",
        1.5,
        [
            pltpu.VMEM((tokens, units), BF16),
            pltpu.VMEM((tokens, units), BF16),
            pltpu.VMEM((tokens, units), F32),
            pltpu.VMEM((tokens, units), F32),
        ]
        + [pltpu.VMEM((tokens, units), BF16)] * (groups - 4)
        + [pltpu.VMEM((tokens, rank), F32)] * groups,
        [VMEM] * (4 + groups),
    )(held, at, own_hidden, held_sums, held_lows, *[theirs[d] for d in reversed(others)])
    own_low, *lows = terms[groups - 4 :]
    back = sum_over_fsdp(back, held_lows, own_low)
    came = [swap(term, "group", d) for d, term in enumerate(terms[: groups - 4], 2)]
    ways = (1, far ^ 1)
    far_term = swap_pair(far_term, ways)
    letters = call(
        letter_kernel,
        "letter",
        0.3,
        [pltpu.VMEM((tokens + tail_rows, 2 * rank), F32)] * (groups - 1),
        [VMEM] * (1 + groups),
    )(back, tail, *lows)
    letters = [swap(letters[d - 1], "group", d) for d in reversed(others)]
    came.append(swap_pair(early, ways))
    (late,) = call(add_kernel, "add", 0.5, [pltpu.VMEM((tokens, units), BF16)], [VMEM] * 2)(late, far_term)
    came.append(swap_pair(late, ways[::-1]))

    share = rank // groups
    ride_rows = max(share, 16)
    *pieces, own_term, coefs, low = call(
        functools.partial(adapter_kernel, groups, length, share),
        "adapter",
        1.0,
        [pltpu.VMEM((ride_rows, units), BF16)] * (groups - 1)
        + [
            pltpu.VMEM((share, units), F32),
            pltpu.VMEM((groups * length, chunks * LANES), F32),
            pltpu.VMEM((tokens, rank), BF16),
        ],
        [VMEM] * (groups + 2),
        scratch=[pltpu.VMEM((rank, units), F32)],
    )(own_low, tail, upstream, *letters)
    arrived = {d: swap(pieces[d - 1], "group", d) for d in reversed(others)}
    gradient_down, loss = call(
        functools.partial(down_kernel, groups, length),
        "down",
        1.0,
        [jax.ShapeDtypeStruct((rank, depth), F32), jax.ShapeDtypeStruct((1, 1), F32)],
        [VMEM] * (3 * groups),
        scratch=[pltpu.VMEM((rank, depth), F32), pltpu.SemaphoreType.DMA((2,))],
        out_specs=[HBM, VMEM],
    )(coefs, back, own_hidden, *letters, *[got[d] for d in reversed(others)], *[theirs[d] for d in reversed(others)])
    projection_output, written = call(
        output_kernel,
        "output",
        1.0,
        [jax.ShapeDtypeStruct((tokens, units), BF16), pltpu.VMEM((8, LANES), F32)],
        [VMEM] * (3 + len(came)),
    )(kept, low, up, *came)
    (gradient_up,) = call(
        gradient_kernel,
        "gradient",
        2.5,
        [jax.ShapeDtypeStruct((share, units), F32)],
        [ANY] + [VMEM] * groups,
    )(written, own_term, *[arrived[d] for d in reversed(others)])
    return (projection_output, gradient_down.T, gradient_up, loss[0])


def solution(mesh):
    return jax.shard_map(
        on_device,
        mesh=mesh,
        in_specs=(
            P("group", None),
            P("group", "fsdp"),
            P("group", None),
            P(None, "fsdp"),
            P("group", "fsdp"),
            P("group", None, None),
            P("group", None, None),
            P("group", None),
            P("group", None),
            P("group", None),
        ),
        out_specs=(P("group", "fsdp"), P("group", None), P("group", "fsdp"), P("group")),
        check_vma=False,
    )
```

```python
import functools

import jax
import jax.numpy as jnp
from jax import lax
from jax.experimental import pallas as pl
from jax.experimental.pallas import tpu as pltpu
from jax.sharding import PartitionSpec as P

COMP = 16


ADAPTER_SCALING = 0.25
SPREAD_FLOOR = 0.16
F32 = jnp.float32
BF16 = jnp.bfloat16
LANES = 128
BLOCK = 8
PEAK_FLOPS, PEAK_BYTES = 1.15e9, 3.6e6
STEP = 512
NT = (((1,), (1,)), ((), ()))
TN = (((0,), (0,)), ((), ()))
VMEM = pl.BlockSpec(memory_space=pltpu.VMEM)
SMEM = pl.BlockSpec(memory_space=pltpu.SMEM)
HBM = pl.BlockSpec(memory_space=pltpu.HBM)
ANY = pl.BlockSpec(memory_space=pl.ANY)


def swap(array, axis, distance):
    size = lax.axis_size(axis)
    return lax.ppermute(array, axis, [(i, i ^ distance) for i in range(size)])


def swap_cores(array, axis, partner):
    size = lax.axis_size(axis)
    return lax.ppermute(array, axis, [(i, i ^ partner[i % 2]) for i in range(size)])


def swap_pair(array, partner):
    groups, size = lax.axis_size("group"), lax.axis_size("fsdp")
    return lax.ppermute(
        array,
        ("group", "fsdp"),
        [(g * size + f, (g ^ partner[f % 2]) * size + f) for g in range(groups) for f in range(size)],
    )


def sum_over_fsdp(partial, loaded, earlier, later):
    size = lax.axis_size("fsdp")
    if size & (size - 1):
        return lax.psum(partial, "fsdp")
    chip = after(partial + swap(partial, "fsdp", 1), loaded)
    if size == 8:
        one = swap_cores(chip, "fsdp", (2, 4))
        chip = after(chip, earlier) + swap(chip, "fsdp", 6)
        return chip + (one + swap(after(one, earlier), "fsdp", 1))
    parts = [chip] + [swap(chip, "fsdp", d) for d in range(2, size, 2)]
    while len(parts) > 1:
        parts = [parts[i] + parts[i + 1] for i in range(0, len(parts), 2)]
    return parts[0]


def after(array, earlier):
    return lax.optimization_barrier((array, earlier))[0]


def call(body, name, cost, outs, ins, scratch=(), out_specs=None):
    return pl.pallas_call(
        body,
        out_shape=outs,
        in_specs=ins,
        out_specs=out_specs or [VMEM] * len(outs),
        scratch_shapes=scratch,
        compiler_params=pltpu.CompilerParams(vmem_limit_bytes=8 << 20),
        cost_estimate=pl.CostEstimate(
            flops=int(cost * PEAK_FLOPS), bytes_accessed=int(cost * PEAK_BYTES), transcendentals=0
        ),
        name=name,
    )


def in_hbm(array):
    return pltpu.with_memory_space_constraint(array, pltpu.HBM)


def positions():
    own, member = lax.axis_index("group"), lax.axis_index("fsdp")
    return own, member, lax.rem(member, 2)


def start_all(pairs, sems, first=0):
    copies = [pltpu.make_async_copy(a, b, sems.at[first + i]) for i, (a, b) in enumerate(pairs)]
    for copy in copies:
        copy.start()
    return copies


def pack_kernel(groups, depth, hidden_ref, old_hbm, reward_hbm, length_hbm, dest_hbm, new_hbm, upstream_hbm, up_hbm, *rest):
    messages, tail_ref = rest[: groups - 1], rest[groups - 1]
    upstream_ref, up_ref, back_ref = rest[groups : groups + 3]
    old_ref, new_ref, reward_ref, length_ref, dest_ref, sems, small_sems = rest[groups + 3 :]
    own, _, core = positions()
    half = depth // 2
    small = [(old_hbm, old_ref), (reward_hbm, reward_ref), (length_hbm, length_ref), (dest_hbm, dest_ref)]
    small = start_all(small + [(new_hbm, new_ref)], small_sems)
    factors = start_all([(upstream_hbm, upstream_ref), (up_hbm, up_ref)], small_sems, 5)
    pairs = []
    for d in reversed(range(1, groups)):
        start = pl.multiple_of((own ^ d) * depth + core * half, LANES)
        pairs.append((hidden_ref.at[:, pl.ds(start, half)], messages[d - 1]))
    copies = start_all(pairs, sems)
    for copy in small:
        copy.wait()
    total, squares = jnp.float32(0), jnp.float32(0)
    for k in range(groups):
        total += reward_ref[0, k]
        squares += reward_ref[0, k] * reward_ref[0, k]
    length = old_ref.shape[2]
    lanes = -(-groups * length // LANES) * LANES
    place = lax.broadcasted_iota(jnp.int32, (1, lanes), 1)
    old, new = (jnp.concatenate([ref[0]] * (lanes // length), axis=1) for ref in (old_ref, new_ref))
    line, reward, count = (jnp.zeros((1, lanes), F32) for _ in range(3))
    for k in range(groups):
        start = dest_ref[0, k] * length
        chosen = (place >= start) & (place < start + length)
        line = jnp.where(chosen, old[k : k + 1], line)
        reward = jnp.where(chosen, reward_ref[0, k], reward)
        count = jnp.where(chosen, length_ref[0, k].astype(F32), count)
    lines = [line, reward, count] + [jnp.full((1, lanes), x, F32) for x in (total, squares)]
    lines.append(jnp.zeros((BLOCK - len(lines), lanes), F32))
    chosen = (place >= own * length) & (place < (own + 1) * length)
    lines.append(jnp.where(chosen, new, 0.0))
    if groups % BLOCK:
        lines.append(jnp.zeros((BLOCK - groups % BLOCK, lanes), F32))
    value = jnp.concatenate(lines, axis=0)
    rows = value.shape[0]
    for i in range(lanes // LANES):
        tail_ref[i * rows : (i + 1) * rows] = value[:, i * LANES : (i + 1) * LANES]
    for copy in factors:
        copy.wait()
    back_ref[...] = lax.dot_general(upstream_ref[...], up_ref[...], NT, preferred_element_type=F32)
    for copy in copies:
        copy.wait()


def load_kernel(hidden_ref, at_hbm, own_hidden, at_ref, sems):
    depth = own_hidden.shape[1]
    mine = hidden_ref.at[:, pl.ds(pl.multiple_of(positions()[0] * depth, LANES), depth)]
    for copy in start_all([(mine, own_hidden), (at_hbm, at_ref)], sems):
        copy.wait()


def whole_rows(half, core, message, other):
    a, b = message[:, :half], other[:, :half]
    first = core == 0
    return jnp.concatenate([jnp.where(first, a, b), jnp.where(first, b, a)], axis=1)


def first_kernel(held_ref, at_ref, own_hidden, *refs):
    *messages, sums_ref, low_ref = refs
    messages = messages[::-1]
    units, depth = held_ref.shape
    half = depth // 2
    mine = pl.ds(pl.multiple_of(positions()[2] * half, LANES), half)
    rows = jnp.concatenate([own_hidden[:, mine]] + [ref[...] for ref in messages], axis=0)
    low_ref[...] = lax.dot_general(rows, at_ref[:, mine], NT, preferred_element_type=F32)
    rows = rows.T
    for start in range(0, units, STEP):
        end = min(start + STEP, units)
        sums_ref[start:end] = jnp.dot(held_ref[start:end, mine], rows, preferred_element_type=F32)


def second_kernel(groups, held_ref, at_ref, own_hidden, sums_ref, low_ref, *refs):
    count = groups - 1
    others, refs = refs[:count][::-1], refs[count:]
    far, early, late, kept, nears, lows = *refs[:4], refs[4 : groups], refs[groups:]
    units, depth = held_ref.shape
    tokens, rank = own_hidden.shape[0], low_ref.shape[1]
    half = depth // 2
    core = positions()[2]
    rest = pl.ds(pl.multiple_of((1 - core) * half, LANES), half)
    rows = jnp.concatenate([own_hidden[:, rest]] + [ref[...] for ref in others], axis=0)
    low = low_ref[...] + lax.dot_general(rows, at_ref[:, rest], NT, preferred_element_type=F32)
    for i, ref in enumerate(lows):
        ref[...] = low[i * tokens : (i + 1) * tokens]
    rows = rows.T
    for start in range(0, units, STEP):
        end = min(start + STEP, units)
        result = sums_ref[start:end] + jnp.dot(held_ref[start:end, rest], rows, preferred_element_type=F32)
        result = result.T
        parts = [result[i * tokens : (i + 1) * tokens] for i in range(groups)]
        kept[:, start:end] = parts[0]
        far[:, start:end] = parts[-1].astype(BF16)
        early[:, start:end] = jnp.where(core == 0, parts[1], parts[-2]).astype(BF16)
        late[:, start:end] = jnp.where(core == 0, parts[-2], parts[1])
        for ref, part in zip(nears, parts[2:-2]):
            ref[:, start:end] = part.astype(BF16)


def add_kernel(late, came, out):
    out[...] = (late[...] + came[...].astype(F32)).astype(BF16)


def letter_kernel(back_ref, tail_ref, *refs):
    count = len(refs) // 2
    tokens, rank = back_ref.shape
    for low, letter in zip(refs[:count], refs[count:]):
        letter[:tokens, :rank] = low[...]
        letter[:tokens, rank:] = back_ref[...]
        letter[tokens:] = tail_ref[...]


def token_coefs(groups, length, tails):
    own = positions()[0]
    chunks = -(-groups * length // LANES)
    rows = tails[0].shape[0] // chunks
    tails = [jnp.concatenate([tail[i * rows : (i + 1) * rows] for i in range(chunks)], axis=1) for tail in tails]
    new = sum(tail[BLOCK : BLOCK + groups] for tail in tails)
    ordered = []
    for j in range(groups):
        table = tails[0][:BLOCK]
        for d in range(1, groups):
            table = jnp.where((own ^ j) == d, tails[d][:BLOCK], table)
        ordered.append(table)
    lanes = new.shape[1]
    place = lax.broadcasted_iota(jnp.int32, (1, lanes), 1)
    together = COMP // groups
    means, squares = [], []
    for j in range(0, groups, together):
        prompt = ordered[j : j + together]
        means += [sum(table[3:4] for table in prompt) / COMP] * together
        squares += [sum(table[4:5] for table in prompt) / COMP] * together
    mean, square = jnp.concatenate(means, axis=0), jnp.concatenate(squares, axis=0)
    old, reward, count = (jnp.concatenate([table[i : i + 1] for table in ordered], axis=0) for i in range(3))
    spread = jnp.sqrt(jnp.maximum(square - mean * mean, SPREAD_FLOOR))
    advantage = (reward - mean) / spread
    ratio = jnp.exp(new - old)
    position = jnp.bitwise_and(place, length - 1).astype(F32)
    live = (position < count) & (place < groups * length)
    coef = jnp.where(live, -(advantage * ratio) / (jnp.maximum(count, 1.0) * COMP), 0.0)
    return jnp.concatenate([jnp.broadcast_to(coef[j : j + 1], (length, lanes)) for j in range(groups)], axis=0)


def coef_column(groups, length, target, coefs):
    row = jnp.concatenate([lax.broadcasted_iota(jnp.int32, (length, coefs.shape[1]), 0)] * groups, axis=0)
    offset = lax.broadcasted_iota(jnp.int32, coefs.shape, 1) - row
    return jnp.sum(jnp.where(offset == target * length, coefs, 0.0), axis=1, keepdims=True)


def adapter_kernel(groups, length, share, own_low, own_tail, upstream_ref, *refs):
    count = groups - 1
    letters, messages, (own_term, coef_ref, low_ref, term) = refs[:count][::-1], refs[count : 2 * count], refs[2 * count :]
    own = positions()[0]
    tokens, rank = own_low.shape
    coefs = token_coefs(groups, length, [own_tail[...]] + [ref[tokens:] for ref in letters])
    coef_ref[...] = coefs
    coef = coef_column(groups, length, own, coefs)
    low = own_low[...]
    for ref in letters:
        low = low + ref[:tokens, :rank]
    low = low.astype(BF16)
    low_ref[...] = low
    gradient = (coef * upstream_ref[...].astype(F32)).astype(BF16)
    term[...] = ADAPTER_SCALING * lax.dot_general(low, gradient, TN, preferred_element_type=F32)
    for d in range(groups):
        if share % BLOCK == 0:
            piece = term[pl.ds(pl.multiple_of((own ^ d) * share, share), share), :]
        else:
            piece = term[:share]
            for j in range(1, groups):
                piece = jnp.where((own ^ d) == j, term[j * share : (j + 1) * share], piece)
        if d == 0:
            own_term[...] = piece
            continue
        rows = messages[d - 1].shape[0]
        if share < rows:
            piece = jnp.concatenate([piece, jnp.zeros((rows - share, piece.shape[1]), F32)], axis=0)
        messages[d - 1][...] = piece.astype(BF16)


def output_kernel(total_ref, low_ref, up_ref, *rest):
    total = total_ref[...] + ADAPTER_SCALING * jnp.dot(low_ref[...], up_ref[...], preferred_element_type=F32)
    for ref in rest[:-2]:
        total = total + ref[...].astype(F32)
    rest[-2][...] = total.astype(BF16)
    rest[-1][...] = jnp.zeros_like(rest[-1])


def down_kernel(groups, length, coef_ref, own_back, own_hidden, *rest):
    count = groups - 1
    letters, messages, others = (rest[i * count : (i + 1) * count][::-1] for i in range(3))
    down_hbm, loss_ref, down_ref, sems = rest[3 * count :]
    own = positions()[0]
    tokens, rank = own_back.shape
    coefs = coef_ref[...]
    backs = [own_back[...]] + [ref[:tokens, rank:] for ref in letters]
    columns = [coef_column(groups, length, own ^ d, coefs) for d in range(groups)]
    loss_ref[...] = jnp.sum(columns[0], axis=0, keepdims=True)
    back = jnp.concatenate([column * part for column, part in zip(columns, backs)], axis=0).astype(BF16)
    core = positions()[2]
    half = own_hidden.shape[1] // 2
    copies = []
    for i in range(2):
        span = slice(i * half, (i + 1) * half)
        rows = [own_hidden[:, span]]
        rows += [jnp.where(core == i, a[...], b[...]) for a, b in zip(messages, others)]
        rows = jnp.concatenate(rows, axis=0)
        down_ref[:, span] = ADAPTER_SCALING * lax.dot_general(back, rows, TN, preferred_element_type=F32)
        copies += start_all([(down_ref.at[:, span], down_hbm.at[:, span])], sems, i)
    for copy in copies:
        copy.wait()


def gradient_kernel(written, own_term, *rest):
    total = own_term[...]
    for come in rest[:-1]:
        total = total + come[...].astype(F32)[: total.shape[0]]
    rest[-1][...] = total


def on_device(
    hidden_input_slots,
    base_weight,
    adapter_a,
    adapter_up_matrix,
    upstream,
    logp_new,
    logp_old,
    rewards,
    comp_lengths,
    assignment,
):
    groups = lax.axis_size("group")
    tokens = hidden_input_slots.shape[0]
    depth, units = base_weight.shape
    half = depth // 2
    rank = adapter_a.shape[1]
    others = range(1, groups)
    at, weight = adapter_a.T, base_weight.T

    length = logp_new.shape[2]
    chunks = -(-groups * length // LANES)
    tail_rows = chunks * (BLOCK + -(-groups // BLOCK) * BLOCK)
    *messages, tail, upstream, up, back = call(
        functools.partial(pack_kernel, groups, depth),
        "pack",
        1.8,
        [pltpu.VMEM((tokens, half), BF16)] * (groups - 1)
        + [
            pltpu.VMEM((tail_rows, LANES), F32),
            pltpu.VMEM((tokens, units), BF16),
            pltpu.VMEM((rank, units), BF16),
            pltpu.VMEM((tokens, rank), F32),
        ],
        [HBM] * 8,
        scratch=[
            pltpu.VMEM(logp_old.shape, F32),
            pltpu.VMEM(logp_new.shape, F32),
            pltpu.SMEM(rewards.shape, F32),
            pltpu.SMEM(comp_lengths.shape, jnp.int32),
            pltpu.SMEM(assignment.shape, jnp.int32),
            pltpu.SemaphoreType.DMA((groups - 1,)),
            pltpu.SemaphoreType.DMA((7,)),
        ],
    )(
        *map(
            in_hbm,
            (
                hidden_input_slots,
                logp_old,
                rewards,
                comp_lengths,
                assignment,
                logp_new,
                upstream,
                adapter_up_matrix,
            ),
        )
    )
    got = {d: swap(messages[d - 1], "group", d) for d in reversed(others)}
    own_hidden, at = call(
        load_kernel,
        "load",
        1.0,
        [pltpu.VMEM((tokens, depth), BF16), pltpu.VMEM((rank, depth), BF16)],
        [HBM] * 2,
        scratch=[pltpu.SemaphoreType.DMA((2,))],
    )(in_hbm(hidden_input_slots), in_hbm(at))
    held = pltpu.with_memory_space_constraint(weight, pltpu.VMEM)
    far, near = groups - 1, list(range(1, groups - 1))
    held_sums, held_lows = call(
        first_kernel,
        "first",
        1.5,
        [pltpu.VMEM((units, groups * tokens), F32), pltpu.VMEM((groups * tokens, rank), F32)],
        [VMEM] * (2 + groups),
    )(held, at, own_hidden, *[got[d] for d in reversed(others)])
    theirs = {d: swap(got[d], "fsdp", 1) for d in reversed(others)}
    far_term, early, late, kept, *terms = call(
        functools.partial(second_kernel, groups),
        "second",
        1.5,
        [
            pltpu.VMEM((tokens, units), BF16),
            pltpu.VMEM((tokens, units), BF16),
            pltpu.VMEM((tokens, units), F32),
            pltpu.VMEM((tokens, units), F32),
        ]
        + [pltpu.VMEM((tokens, units), BF16)] * (groups - 4)
        + [pltpu.VMEM((tokens, rank), F32)] * groups,
        [VMEM] * (4 + groups),
    )(held, at, own_hidden, held_sums, held_lows, *[theirs[d] for d in reversed(others)])
    own_low, *lows = terms[groups - 4 :]
    back = sum_over_fsdp(back, at, held_lows, own_low)
    came = [swap(term, "group", d) for d, term in enumerate(terms[: groups - 4], 2)]
    ways = (1, far ^ 1)
    far_term = swap_pair(far_term, ways)
    letters = call(
        letter_kernel,
        "letter",
        0.3,
        [pltpu.VMEM((tokens + tail_rows, 2 * rank), F32)] * (groups - 1),
        [VMEM] * (1 + groups),
    )(back, tail, *lows)
    letters = [swap(letters[d - 1], "group", d) for d in reversed(others)]
    came.append(swap_pair(early, ways))
    (late,) = call(add_kernel, "add", 0.5, [pltpu.VMEM((tokens, units), BF16)], [VMEM] * 2)(late, far_term)
    came.append(swap_pair(late, ways[::-1]))

    share = rank // groups
    ride_rows = max(share, 16)
    *pieces, own_term, coefs, low = call(
        functools.partial(adapter_kernel, groups, length, share),
        "adapter",
        1.0,
        [pltpu.VMEM((ride_rows, units), BF16)] * (groups - 1)
        + [
            pltpu.VMEM((share, units), F32),
            pltpu.VMEM((groups * length, chunks * LANES), F32),
            pltpu.VMEM((tokens, rank), BF16),
        ],
        [VMEM] * (groups + 2),
        scratch=[pltpu.VMEM((rank, units), F32)],
    )(own_low, tail, upstream, *letters)
    arrived = {d: swap(pieces[d - 1], "group", d) for d in reversed(others)}
    gradient_down, loss = call(
        functools.partial(down_kernel, groups, length),
        "down",
        1.0,
        [jax.ShapeDtypeStruct((rank, depth), F32), jax.ShapeDtypeStruct((1, 1), F32)],
        [VMEM] * (3 * groups),
        scratch=[pltpu.VMEM((rank, depth), F32), pltpu.SemaphoreType.DMA((2,))],
        out_specs=[HBM, VMEM],
    )(coefs, back, own_hidden, *letters, *[got[d] for d in reversed(others)], *[theirs[d] for d in reversed(others)])
    projection_output, written = call(
        output_kernel,
        "output",
        1.0,
        [jax.ShapeDtypeStruct((tokens, units), BF16), pltpu.VMEM((8, LANES), F32)],
        [VMEM] * (3 + len(came)),
    )(kept, low, up, *came)
    (gradient_up,) = call(
        gradient_kernel,
        "gradient",
        2.5,
        [jax.ShapeDtypeStruct((share, units), F32)],
        [ANY] + [VMEM] * groups,
    )(written, own_term, *[arrived[d] for d in reversed(others)])
    return (projection_output, gradient_down.T, gradient_up, loss[0])


def solution(mesh):
    return jax.shard_map(
        on_device,
        mesh=mesh,
        in_specs=(
            P("group", None),
            P("group", "fsdp"),
            P("group", None),
            P(None, "fsdp"),
            P("group", "fsdp"),
            P("group", None, None),
            P("group", None, None),
            P("group", None),
            P("group", None),
            P("group", None),
        ),
        out_specs=(P("group", "fsdp"), P("group", None), P("group", "fsdp"), P("group")),
        check_vma=False,
    )
```

```python
import functools

import jax
import jax.numpy as jnp
from jax import lax
from jax.experimental import pallas as pl
from jax.experimental.pallas import tpu as pltpu
from jax.sharding import PartitionSpec as P

COMP = 16


ADAPTER_SCALING = 0.25
SPREAD_FLOOR = 0.16
F32 = jnp.float32
BF16 = jnp.bfloat16
LANES = 128
BLOCK = 8
PEAK_FLOPS, PEAK_BYTES = 1.15e9, 3.6e6
STEP = 512
NT = (((1,), (1,)), ((), ()))
TN = (((0,), (0,)), ((), ()))
VMEM = pl.BlockSpec(memory_space=pltpu.VMEM)
SMEM = pl.BlockSpec(memory_space=pltpu.SMEM)
HBM = pl.BlockSpec(memory_space=pltpu.HBM)
ANY = pl.BlockSpec(memory_space=pl.ANY)


def swap(array, axis, distance):
    size = lax.axis_size(axis)
    return lax.ppermute(array, axis, [(i, i ^ distance) for i in range(size)])


def swap_cores(array, axis, partner):
    size = lax.axis_size(axis)
    return lax.ppermute(array, axis, [(i, i ^ partner[i % 2]) for i in range(size)])


def swap_pair(array, partner):
    groups, size = lax.axis_size("group"), lax.axis_size("fsdp")
    return lax.ppermute(
        array,
        ("group", "fsdp"),
        [(g * size + f, (g ^ partner[f % 2]) * size + f) for g in range(groups) for f in range(size)],
    )


def sum_over_fsdp(partial, loaded, earlier, later):
    size = lax.axis_size("fsdp")
    if size & (size - 1):
        return lax.psum(partial, "fsdp")
    chip = after(partial + swap(partial, "fsdp", 1), loaded)
    if size == 8:
        one = swap_cores(chip, "fsdp", (2, 4))
        chip = after(chip, earlier) + swap(chip, "fsdp", 6)
        return chip + (one + swap(after(one, earlier), "fsdp", 1))
    parts = [chip] + [swap(chip, "fsdp", d) for d in range(2, size, 2)]
    while len(parts) > 1:
        parts = [parts[i] + parts[i + 1] for i in range(0, len(parts), 2)]
    return parts[0]


def after(array, earlier):
    return lax.optimization_barrier((array, earlier))[0]


def call(body, name, cost, outs, ins, scratch=(), out_specs=None):
    return pl.pallas_call(
        body,
        out_shape=outs,
        in_specs=ins,
        out_specs=out_specs or [VMEM] * len(outs),
        scratch_shapes=scratch,
        compiler_params=pltpu.CompilerParams(vmem_limit_bytes=8 << 20),
        cost_estimate=pl.CostEstimate(
            flops=int(cost * PEAK_FLOPS), bytes_accessed=int(cost * PEAK_BYTES), transcendentals=0
        ),
        name=name,
    )


def in_hbm(array):
    return pltpu.with_memory_space_constraint(array, pltpu.HBM)


def positions():
    own, member = lax.axis_index("group"), lax.axis_index("fsdp")
    return own, member, lax.rem(member, 2)


def start_all(pairs, sems, first=0):
    copies = [pltpu.make_async_copy(a, b, sems.at[first + i]) for i, (a, b) in enumerate(pairs)]
    for copy in copies:
        copy.start()
    return copies


def pack_kernel(groups, depth, hidden_ref, old_hbm, reward_hbm, length_hbm, dest_hbm, new_hbm, upstream_hbm, up_hbm, *rest):
    messages, tail_ref = rest[: groups - 1], rest[groups - 1]
    upstream_ref, up_ref, back_ref = rest[groups : groups + 3]
    old_ref, new_ref, reward_ref, length_ref, dest_ref, sems, small_sems = rest[groups + 3 :]
    own, _, core = positions()
    half = depth // 2
    small = [(old_hbm, old_ref), (reward_hbm, reward_ref), (length_hbm, length_ref), (dest_hbm, dest_ref)]
    small = start_all(small + [(new_hbm, new_ref)], small_sems)
    factors = start_all([(upstream_hbm, upstream_ref), (up_hbm, up_ref)], small_sems, 5)
    pairs = []
    for d in reversed(range(1, groups)):
        start = pl.multiple_of((own ^ d) * depth + core * half, LANES)
        pairs.append((hidden_ref.at[:, pl.ds(start, half)], messages[d - 1]))
    copies = start_all(pairs, sems)
    for copy in small:
        copy.wait()
    total, squares = jnp.float32(0), jnp.float32(0)
    for k in range(groups):
        total += reward_ref[0, k]
        squares += reward_ref[0, k] * reward_ref[0, k]
    length = old_ref.shape[2]
    lanes = -(-groups * length // LANES) * LANES
    place = lax.broadcasted_iota(jnp.int32, (1, lanes), 1)
    old, new = (jnp.concatenate([ref[0]] * (lanes // length), axis=1) for ref in (old_ref, new_ref))
    line, reward, count = (jnp.zeros((1, lanes), F32) for _ in range(3))
    for k in range(groups):
        start = dest_ref[0, k] * length
        chosen = (place >= start) & (place < start + length)
        line = jnp.where(chosen, old[k : k + 1], line)
        reward = jnp.where(chosen, reward_ref[0, k], reward)
        count = jnp.where(chosen, length_ref[0, k].astype(F32), count)
    lines = [line, reward, count] + [jnp.full((1, lanes), x, F32) for x in (total, squares)]
    lines.append(jnp.zeros((BLOCK - len(lines), lanes), F32))
    chosen = (place >= own * length) & (place < (own + 1) * length)
    lines.append(jnp.where(chosen, new, 0.0))
    if groups % BLOCK:
        lines.append(jnp.zeros((BLOCK - groups % BLOCK, lanes), F32))
    value = jnp.concatenate(lines, axis=0)
    rows = value.shape[0]
    for i in range(lanes // LANES):
        tail_ref[i * rows : (i + 1) * rows] = value[:, i * LANES : (i + 1) * LANES]
    for copy in factors:
        copy.wait()
    back_ref[...] = lax.dot_general(upstream_ref[...], up_ref[...], NT, preferred_element_type=F32)
    for copy in copies:
        copy.wait()


def load_kernel(hidden_ref, at_hbm, own_hidden, at_ref, sems):
    depth = own_hidden.shape[1]
    mine = hidden_ref.at[:, pl.ds(pl.multiple_of(positions()[0] * depth, LANES), depth)]
    for copy in start_all([(mine, own_hidden), (at_hbm, at_ref)], sems):
        copy.wait()


def whole_rows(half, core, message, other):
    a, b = message[:, :half], other[:, :half]
    first = core == 0
    return jnp.concatenate([jnp.where(first, a, b), jnp.where(first, b, a)], axis=1)


def first_kernel(held_ref, at_ref, own_hidden, *refs):
    *messages, sums_ref, low_ref = refs
    messages = messages[::-1]
    units, depth = held_ref.shape
    half = depth // 2
    mine = pl.ds(pl.multiple_of(positions()[2] * half, LANES), half)
    rows = jnp.concatenate([own_hidden[:, mine]] + [ref[...] for ref in messages], axis=0)
    low_ref[...] = lax.dot_general(rows, at_ref[:, mine], NT, preferred_element_type=F32)
    rows = rows.T
    for start in range(0, units, STEP):
        end = min(start + STEP, units)
        sums_ref[start:end] = jnp.dot(held_ref[start:end, mine], rows, preferred_element_type=F32)


def second_kernel(groups, held_ref, at_ref, own_hidden, sums_ref, low_ref, *refs):
    count = groups - 1
    others, refs = refs[:count][::-1], refs[count:]
    far, early, late, kept, nears, lows = *refs[:4], refs[4 : groups], refs[groups:]
    units, depth = held_ref.shape
    tokens, rank = own_hidden.shape[0], low_ref.shape[1]
    half = depth // 2
    core = positions()[2]
    rest = pl.ds(pl.multiple_of((1 - core) * half, LANES), half)
    rows = jnp.concatenate([own_hidden[:, rest]] + [ref[...] for ref in others], axis=0)
    low = low_ref[...] + lax.dot_general(rows, at_ref[:, rest], NT, preferred_element_type=F32)
    for i, ref in enumerate(lows):
        ref[...] = low[i * tokens : (i + 1) * tokens]
    rows = rows.T
    for start in range(0, units, STEP):
        end = min(start + STEP, units)
        result = sums_ref[start:end] + jnp.dot(held_ref[start:end, rest], rows, preferred_element_type=F32)
        result = result.T
        parts = [result[i * tokens : (i + 1) * tokens] for i in range(groups)]
        kept[:, start:end] = parts[0]
        far[:, start:end] = parts[-1].astype(BF16)
        early[:, start:end] = jnp.where(core == 0, parts[-2], parts[1]).astype(BF16)
        late[:, start:end] = jnp.where(core == 0, parts[1], parts[-2])
        for ref, part in zip(nears, parts[2:-2]):
            ref[:, start:end] = part.astype(BF16)


def add_kernel(late, came, out):
    out[...] = (late[...] + came[...].astype(F32)).astype(BF16)


def letter_kernel(back_ref, tail_ref, *refs):
    count = len(refs) // 2
    tokens, rank = back_ref.shape
    for low, letter in zip(refs[:count], refs[count:]):
        letter[:tokens, :rank] = low[...]
        letter[:tokens, rank:] = back_ref[...]
        letter[tokens:] = tail_ref[...]


def token_coefs(groups, length, tails):
    own = positions()[0]
    chunks = -(-groups * length // LANES)
    rows = tails[0].shape[0] // chunks
    tails = [jnp.concatenate([tail[i * rows : (i + 1) * rows] for i in range(chunks)], axis=1) for tail in tails]
    new = sum(tail[BLOCK : BLOCK + groups] for tail in tails)
    ordered = []
    for j in range(groups):
        table = tails[0][:BLOCK]
        for d in range(1, groups):
            table = jnp.where((own ^ j) == d, tails[d][:BLOCK], table)
        ordered.append(table)
    lanes = new.shape[1]
    place = lax.broadcasted_iota(jnp.int32, (1, lanes), 1)
    together = COMP // groups
    means, squares = [], []
    for j in range(0, groups, together):
        prompt = ordered[j : j + together]
        means += [sum(table[3:4] for table in prompt) / COMP] * together
        squares += [sum(table[4:5] for table in prompt) / COMP] * together
    mean, square = jnp.concatenate(means, axis=0), jnp.concatenate(squares, axis=0)
    old, reward, count = (jnp.concatenate([table[i : i + 1] for table in ordered], axis=0) for i in range(3))
    spread = jnp.sqrt(jnp.maximum(square - mean * mean, SPREAD_FLOOR))
    advantage = (reward - mean) / spread
    ratio = jnp.exp(new - old)
    position = jnp.bitwise_and(place, length - 1).astype(F32)
    live = (position < count) & (place < groups * length)
    coef = jnp.where(live, -(advantage * ratio) / (jnp.maximum(count, 1.0) * COMP), 0.0)
    return jnp.concatenate([jnp.broadcast_to(coef[j : j + 1], (length, lanes)) for j in range(groups)], axis=0)


def coef_column(groups, length, target, coefs):
    row = jnp.concatenate([lax.broadcasted_iota(jnp.int32, (length, coefs.shape[1]), 0)] * groups, axis=0)
    offset = lax.broadcasted_iota(jnp.int32, coefs.shape, 1) - row
    return jnp.sum(jnp.where(offset == target * length, coefs, 0.0), axis=1, keepdims=True)


def adapter_kernel(groups, length, share, own_low, own_tail, upstream_ref, *refs):
    count = groups - 1
    letters, messages, (own_term, coef_ref, low_ref, term) = refs[:count][::-1], refs[count : 2 * count], refs[2 * count :]
    own = positions()[0]
    tokens, rank = own_low.shape
    coefs = token_coefs(groups, length, [own_tail[...]] + [ref[tokens:] for ref in letters])
    coef_ref[...] = coefs
    coef = coef_column(groups, length, own, coefs)
    low = own_low[...]
    for ref in letters:
        low = low + ref[:tokens, :rank]
    low = low.astype(BF16)
    low_ref[...] = low
    gradient = (coef * upstream_ref[...].astype(F32)).astype(BF16)
    term[...] = ADAPTER_SCALING * lax.dot_general(low, gradient, TN, preferred_element_type=F32)
    for d in range(groups):
        if share % BLOCK == 0:
            piece = term[pl.ds(pl.multiple_of((own ^ d) * share, share), share), :]
        else:
            piece = term[:share]
            for j in range(1, groups):
                piece = jnp.where((own ^ d) == j, term[j * share : (j + 1) * share], piece)
        if d == 0:
            own_term[...] = piece
            continue
        rows = messages[d - 1].shape[0]
        if share < rows:
            piece = jnp.concatenate([piece, jnp.zeros((rows - share, piece.shape[1]), F32)], axis=0)
        messages[d - 1][...] = piece.astype(BF16)


def output_kernel(total_ref, low_ref, up_ref, *rest):
    total = total_ref[...] + ADAPTER_SCALING * jnp.dot(low_ref[...], up_ref[...], preferred_element_type=F32)
    for ref in rest[:-2]:
        total = total + ref[...].astype(F32)
    rest[-2][...] = total.astype(BF16)
    rest[-1][...] = jnp.zeros_like(rest[-1])


def down_kernel(groups, length, coef_ref, own_back, own_hidden, *rest):
    count = groups - 1
    letters, messages, others = (rest[i * count : (i + 1) * count][::-1] for i in range(3))
    down_hbm, loss_ref, down_ref, sems = rest[3 * count :]
    own = positions()[0]
    tokens, rank = own_back.shape
    coefs = coef_ref[...]
    backs = [own_back[...]] + [ref[:tokens, rank:] for ref in letters]
    columns = [coef_column(groups, length, own ^ d, coefs) for d in range(groups)]
    loss_ref[...] = jnp.sum(columns[0], axis=0, keepdims=True)
    back = jnp.concatenate([column * part for column, part in zip(columns, backs)], axis=0).astype(BF16)
    core = positions()[2]
    half = own_hidden.shape[1] // 2
    copies = []
    for i in range(2):
        span = slice(i * half, (i + 1) * half)
        rows = [own_hidden[:, span]]
        rows += [jnp.where(core == i, a[...], b[...]) for a, b in zip(messages, others)]
        rows = jnp.concatenate(rows, axis=0)
        down_ref[:, span] = ADAPTER_SCALING * lax.dot_general(back, rows, TN, preferred_element_type=F32)
        copies += start_all([(down_ref.at[:, span], down_hbm.at[:, span])], sems, i)
    for copy in copies:
        copy.wait()


def gradient_kernel(written, own_term, *rest):
    total = own_term[...]
    for come in rest[:-1]:
        total = total + come[...].astype(F32)[: total.shape[0]]
    rest[-1][...] = total


def on_device(
    hidden_input_slots,
    base_weight,
    adapter_a,
    adapter_up_matrix,
    upstream,
    logp_new,
    logp_old,
    rewards,
    comp_lengths,
    assignment,
):
    groups = lax.axis_size("group")
    tokens = hidden_input_slots.shape[0]
    depth, units = base_weight.shape
    half = depth // 2
    rank = adapter_a.shape[1]
    others = range(1, groups)
    at, weight = adapter_a.T, base_weight.T

    length = logp_new.shape[2]
    chunks = -(-groups * length // LANES)
    tail_rows = chunks * (BLOCK + -(-groups // BLOCK) * BLOCK)
    *messages, tail, upstream, up, back = call(
        functools.partial(pack_kernel, groups, depth),
        "pack",
        1.8,
        [pltpu.VMEM((tokens, half), BF16)] * (groups - 1)
        + [
            pltpu.VMEM((tail_rows, LANES), F32),
            pltpu.VMEM((tokens, units), BF16),
            pltpu.VMEM((rank, units), BF16),
            pltpu.VMEM((tokens, rank), F32),
        ],
        [HBM] * 8,
        scratch=[
            pltpu.VMEM(logp_old.shape, F32),
            pltpu.VMEM(logp_new.shape, F32),
            pltpu.SMEM(rewards.shape, F32),
            pltpu.SMEM(comp_lengths.shape, jnp.int32),
            pltpu.SMEM(assignment.shape, jnp.int32),
            pltpu.SemaphoreType.DMA((groups - 1,)),
            pltpu.SemaphoreType.DMA((7,)),
        ],
    )(
        *map(
            in_hbm,
            (
                hidden_input_slots,
                logp_old,
                rewards,
                comp_lengths,
                assignment,
                logp_new,
                upstream,
                adapter_up_matrix,
            ),
        )
    )
    got = {d: swap(messages[d - 1], "group", d) for d in reversed(others)}
    own_hidden, at = call(
        load_kernel,
        "load",
        1.0,
        [pltpu.VMEM((tokens, depth), BF16), pltpu.VMEM((rank, depth), BF16)],
        [HBM] * 2,
        scratch=[pltpu.SemaphoreType.DMA((2,))],
    )(in_hbm(hidden_input_slots), in_hbm(at))
    held = pltpu.with_memory_space_constraint(weight, pltpu.VMEM)
    far, near = groups - 1, list(range(1, groups - 1))
    held_sums, held_lows = call(
        first_kernel,
        "first",
        1.5,
        [pltpu.VMEM((units, groups * tokens), F32), pltpu.VMEM((groups * tokens, rank), F32)],
        [VMEM] * (2 + groups),
    )(held, at, own_hidden, *[got[d] for d in reversed(others)])
    theirs = {d: swap(got[d], "fsdp", 1) for d in reversed(others)}
    far_term, early, late, kept, *terms = call(
        functools.partial(second_kernel, groups),
        "second",
        1.5,
        [
            pltpu.VMEM((tokens, units), BF16),
            pltpu.VMEM((tokens, units), BF16),
            pltpu.VMEM((tokens, units), F32),
            pltpu.VMEM((tokens, units), F32),
        ]
        + [pltpu.VMEM((tokens, units), BF16)] * (groups - 4)
        + [pltpu.VMEM((tokens, rank), F32)] * groups,
        [VMEM] * (4 + groups),
    )(held, at, own_hidden, held_sums, held_lows, *[theirs[d] for d in reversed(others)])
    own_low, *lows = terms[groups - 4 :]
    back = sum_over_fsdp(back, at, held_lows, own_low)
    came = [swap(term, "group", d) for d, term in enumerate(terms[: groups - 4], 2)]
    ways = (far ^ 1, 1)
    far_term = swap_pair(far_term, ways)
    letters = call(
        letter_kernel,
        "letter",
        0.3,
        [pltpu.VMEM((tokens + tail_rows, 2 * rank), F32)] * (groups - 1),
        [VMEM] * (1 + groups),
    )(back, tail, *lows)
    letters = [swap(letters[d - 1], "group", d) for d in reversed(others)]
    came.append(swap_pair(early, ways))
    (late,) = call(add_kernel, "add", 0.5, [pltpu.VMEM((tokens, units), BF16)], [VMEM] * 2)(late, far_term)
    came.append(swap_pair(late, ways[::-1]))

    share = rank // groups
    ride_rows = max(share, 16)
    *pieces, own_term, coefs, low = call(
        functools.partial(adapter_kernel, groups, length, share),
        "adapter",
        1.0,
        [pltpu.VMEM((ride_rows, units), BF16)] * (groups - 1)
        + [
            pltpu.VMEM((share, units), F32),
            pltpu.VMEM((groups * length, chunks * LANES), F32),
            pltpu.VMEM((tokens, rank), BF16),
        ],
        [VMEM] * (groups + 2),
        scratch=[pltpu.VMEM((rank, units), F32)],
    )(own_low, tail, upstream, *letters)
    arrived = {d: swap(pieces[d - 1], "group", d) for d in reversed(others)}
    gradient_down, loss = call(
        functools.partial(down_kernel, groups, length),
        "down",
        1.0,
        [jax.ShapeDtypeStruct((rank, depth), F32), jax.ShapeDtypeStruct((1, 1), F32)],
        [VMEM] * (3 * groups),
        scratch=[pltpu.VMEM((rank, depth), F32), pltpu.SemaphoreType.DMA((2,))],
        out_specs=[HBM, VMEM],
    )(coefs, back, own_hidden, *letters, *[got[d] for d in reversed(others)], *[theirs[d] for d in reversed(others)])
    projection_output, written = call(
        output_kernel,
        "output",
        1.0,
        [jax.ShapeDtypeStruct((tokens, units), BF16), pltpu.VMEM((8, LANES), F32)],
        [VMEM] * (3 + len(came)),
    )(kept, low, up, *came)
    (gradient_up,) = call(
        gradient_kernel,
        "gradient",
        2.5,
        [jax.ShapeDtypeStruct((share, units), F32)],
        [ANY] + [VMEM] * groups,
    )(written, own_term, *[arrived[d] for d in reversed(others)])
    return (projection_output, gradient_down.T, gradient_up, loss[0])


def solution(mesh):
    return jax.shard_map(
        on_device,
        mesh=mesh,
        in_specs=(
            P("group", None),
            P("group", "fsdp"),
            P("group", None),
            P(None, "fsdp"),
            P("group", "fsdp"),
            P("group", None, None),
            P("group", None, None),
            P("group", None),
            P("group", None),
            P("group", None),
        ),
        out_specs=(P("group", "fsdp"), P("group", None), P("group", "fsdp"), P("group")),
        check_vma=False,
    )
```
